256 devices in a mesh: chan: 64 (over x, z, core), src: 4 (over y).
Axes of the slice: x: 4, y: 4, z: 8, core: 2. Of those that a mesh axis runs over, the one named last changes fastest.
Arguments:
- records: bfloat16 [8192, 4096], P('chan'), may hold values from -600 to 600
- virtual_sources: int32 [64], P('src'), may hold values from 0 to 8191
- pair_group: int32 [32768, 1], P(('chan', 'src')), may hold values from 0 to 63; in each aligned block of 128 rows (0 to 127, 128 to 255, ...) at most 4 rows name the same one
- pair_receiver: int32 [32768], P(('chan', 'src')), may hold values from 0 to 127
- pair_source: int32 [32768], P(('chan', 'src')), may hold values from 0 to 15
- observed: float32 [32768, 2048], P(('chan', 'src')), may hold values from -6 to 6
Outputs:
- adjoint_source: float32 [8192, 4096], P(('chan', 'src'))
- pair_misfit: float32 [32768], P(('chan', 'src'))
The draws below stay inside these ranges and needn't reach their ends.
Inputs may be any that keep to these rules, and one draw needn't show every extreme that they name: `pair_group`: among the 128 pairs listed by one device at most 4 name the same channel group, and in every draw some device lists exactly 4 pairs for some group.
All inputs are finite; a program needn't handle non-finite values.
Results may differ from the reference program's by a relative error of at most 0.0021.
Values sent between devices are 32-bit elements; how exact they have to be, the bound alone decides.
A program may use at most 64 MiB of HBM per device.

```python
import math
import jax
import jax.numpy as jnp
import numpy as np
from jax import lax

NT = 4096
NF = 1024
K0 = 64
CH_DEV = 128
SRC_DEV = 16
PAIR_DEV = 128
CHANNELS = 8192
NSRC = 64
PAIRS = 32768
CAP = 4
N_CHAN = 64
N_SRC = 4


def draw_records(key, part):
    key_base, key_rows, key_times = jax.random.split(key, 3)
    base_values = jnp.clip(jax.random.normal(key_base, (CHANNELS, NT), jnp.float32), -6.0, 6.0)
    row_scale = jnp.exp(jax.random.uniform(key_rows, (CHANNELS, 1), jnp.float32, 0.0, math.log(10.0)))
    time_scale = jnp.exp(jax.random.uniform(key_times, (1, NT), jnp.float32, 0.0, math.log(10.0)))
    return jnp.clip(base_values * row_scale * time_scale, -600.0, 600.0).astype(jnp.bfloat16)


def set_ends(drawn, key, smallest, largest):
    extent = drawn.shape
    place = [jax.random.randint(jax.random.fold_in(key, axis), (), 0, extent[axis]) for axis in range(len(extent))]
    drawn = drawn.at[tuple(place)].set(smallest)
    longest = extent.index(max(extent))
    place[longest] = (place[longest] + 1) % extent[longest]
    return drawn.at[tuple(place)].set(largest)


def levels(rng, dims, cuts, smallest, top_value):
    gain, own = 1.0, jax.random.fold_in(rng, 6)
    for position, blocks in cuts:
        heights = jnp.exp(jax.random.uniform(jax.random.fold_in(own, position), (blocks,), jnp.float32, smallest / len(cuts), top_value / len(cuts)))
        gain = gain * jnp.repeat(heights, dims[position] // blocks).reshape([-1 if axis == position else 1 for axis in range(len(dims))])
    return gain


def routed_block(rng, own, number, rows, amount, top, reach, slope):
    order = jax.random.permutation(rng, amount)
    crowded, common = portions_of(amount, rows * top, reach, slope, True), portions_of(amount, rows * top, reach, slope, False)
    places = jnp.arange(amount)

    def named(sizes, turn):
        used = int((sizes > 0).sum())
        fixed = max(1, used // 4)
        passed = fixed + (places - fixed + turn * (used - fixed)) % max(1, amount - fixed)
        return jnp.zeros((amount,), jnp.int32).at[order[jnp.where(places < fixed, places, passed)]].set(jnp.asarray(sizes, jnp.int32))

    sizes = jnp.where(number % 4 == 0, named(crowded, number // 4), named(common, number - number // 4 - 1))
    mixed = jax.random.permutation(jax.random.fold_in(own, 3), amount)
    giver, receiver = mixed[0:amount // 2 * 2:2], mixed[1:amount // 2 * 2:2]
    margin = jnp.minimum(sizes[giver] - 1, reach - sizes[receiver]) // 2
    margin = jnp.where((giver == order[0]) | (receiver == order[0]) | (sizes[receiver] == 0), 0, jnp.maximum(margin, 0))
    passed = jax.random.randint(jax.random.fold_in(own, 4), (amount // 2,), 0, 1 << 20) % (margin + 1)
    sizes = sizes.at[giver].add(-passed).at[receiver].add(passed)
    items = jnp.searchsorted(jnp.cumsum(sizes), jnp.arange(rows * top), side="right").astype(jnp.int32)
    table = items.reshape(top, rows).T
    table = table[jax.random.permutation(jax.random.fold_in(own, 1), rows)]
    turn = jax.random.randint(jax.random.fold_in(own, 2), (rows, 1), 0, top)
    return jnp.take_along_axis(table, (jnp.arange(top)[None, :] + turn) % top, axis=1)


def portions_of(count, total, bound, lean, full):
    loads = [(1 << 20) // math.isqrt(grade ** lean) + 1 for grade in range(1, count + 1)]
    largest = bound if full else min(bound, max(-(-total // count), total * loads[0] // sum(loads)))
    least = 1 if total - largest >= count - 1 else 0
    counts, rest = [largest] + [least] * (count - 1), total - largest - least * (count - 1)
    while rest > 0:
        movable = [i for i in range(1, count) if counts[i] < largest] or [i for i in range(1, count) if counts[i] < bound]
        mass, left = sum([loads[i] for i in movable]), rest
        for i in movable:
            more = min(bound - counts[i], max(1, left * loads[i] // mass), rest)
            counts[i] = counts[i] + more
            rest = rest - more
    return np.array(counts)


def scatter_about(own_key, dims, deviation, bound, shards=(), held_as=jnp.bfloat16):
    entries = deviation * jax.random.normal(own_key, dims, jnp.float32)
    if shards:
        entries = entries * levels(own_key, dims, shards, -0.22, 0.18)
    return jnp.clip(entries, -bound, bound).astype(held_as)


def setup_inputs(seed: int = 0) -> dict:
    key_of = jax.random.split(jax.random.key(seed), 7)
    records = draw_records(jax.random.fold_in(key_of[6], 71), 0)
    virtual_sources = set_ends(jax.random.randint(key_of[1], (NSRC,), 0, CHANNELS), jax.random.fold_in(key_of[1], 1), 0, CHANNELS - 1).astype(jnp.int32)
    pair_group_keys = jax.random.split(jax.random.fold_in(key_of[2], 1), PAIRS // PAIR_DEV)
    pair_group_turns = jax.random.permutation(jax.random.fold_in(key_of[2], 3), PAIRS // PAIR_DEV)
    pair_group = jax.vmap(lambda own, number: routed_block(jax.random.fold_in(key_of[2], 2), own, number, PAIR_DEV, N_CHAN, 1, CAP, 2))(pair_group_keys, pair_group_turns).reshape((PAIRS, 1))
    pair_receiver = set_ends(jax.random.randint(key_of[3], (PAIRS,), 0, CH_DEV), jax.random.fold_in(key_of[3], 1), 0, CH_DEV - 1).astype(jnp.int32)
    pair_source = set_ends(jax.random.randint(key_of[4], (PAIRS,), 0, SRC_DEV), jax.random.fold_in(key_of[4], 1), 0, SRC_DEV - 1).astype(jnp.int32)
    observed = scatter_about(key_of[5], (PAIRS, 2 * NF), 1.0, 6.0, ((0, 256),), jnp.float32)
    return dict(records=records, virtual_sources=virtual_sources, pair_group=pair_group, pair_receiver=pair_receiver, pair_source=pair_source, observed=observed)


def fourier_basis(offset, length):
    sample_times = offset + jnp.arange(length, dtype=jnp.int32)[:, None]
    band_bins = K0 + jnp.arange(NF, dtype=jnp.int32)[None, :]
    phase_index = band_bins * sample_times % (2 * NT)
    angles = phase_index.astype(jnp.float32) * (math.pi / NT)
    return jnp.concatenate([jnp.cos(angles), -jnp.sin(angles)], axis=1)

def whiten(spectra):
    band_power = lax.optimization_barrier(jnp.sum(spectra * spectra, axis=1, keepdims=True)) / NF
    return spectra / jnp.sqrt(band_power + 1e-06)

def band_taper(bin_count):
    band_bins = jnp.arange(bin_count, dtype=jnp.int32).astype(jnp.float32)
    return 0.5 - 0.5 * jnp.cos((band_bins + 0.5) * (2.0 * math.pi / bin_count))

def pair_terms(source_rows, receiver_rows, observed_rows):
    bin_count = observed_rows.shape[-1] // 2
    weights = band_taper(bin_count)
    source_real = source_rows[..., :bin_count]
    source_imag = source_rows[..., bin_count:]
    receiver_real = receiver_rows[..., :bin_count]
    receiver_imag = receiver_rows[..., bin_count:]
    corr_real = source_real * receiver_real + source_imag * receiver_imag
    corr_imag = source_real * receiver_imag - source_imag * receiver_real
    diff_real = corr_real - observed_rows[..., :bin_count]
    diff_imag = corr_imag - observed_rows[..., bin_count:]
    misfit = lax.optimization_barrier(jnp.sum(weights * (diff_real * diff_real + diff_imag * diff_imag), axis=-1)) / (2 * bin_count)
    resid_real = weights * diff_real
    resid_imag = weights * diff_imag
    term_real = resid_real * source_real - resid_imag * source_imag
    term_imag = resid_real * source_imag + resid_imag * source_real
    return (misfit, jnp.concatenate([term_real, term_imag], axis=-1))

def reference(records, virtual_sources, pair_group, pair_receiver, pair_source, observed):
    fourier_table = fourier_basis(0, NT)
    spectra = jnp.dot(records, fourier_table.astype(jnp.bfloat16), preferred_element_type=jnp.float32)
    whitened = whiten(spectra)
    sources = jnp.take(whitened, virtual_sources, axis=0)
    listing = jnp.arange(PAIRS, dtype=jnp.int32)
    source_index = listing // PAIR_DEV % N_SRC * SRC_DEV + pair_source
    receiver_index = pair_group[:, 0] * CH_DEV + pair_receiver

    def one_block(adjoint, block_index):
        offset = (block_index * PAIR_DEV).astype(jnp.int32)
        source_block = lax.dynamic_slice_in_dim(source_index, offset, PAIR_DEV)
        receiver_block = lax.dynamic_slice_in_dim(receiver_index, offset, PAIR_DEV)
        observed_block = lax.dynamic_slice_in_dim(observed, offset, PAIR_DEV, 0)
        misfit, adjoint_term = pair_terms(jnp.take(sources, source_block, axis=0), jnp.take(whitened, receiver_block, axis=0), observed_block)
        return (adjoint.at[receiver_block].add(adjoint_term), misfit)
    adjoint_spectra, misfits = lax.scan(one_block, jnp.zeros((CHANNELS, 2 * NF), jnp.float32), jnp.arange(PAIRS // PAIR_DEV, dtype=jnp.int32))
    adjoint_source = jnp.dot(adjoint_spectra, fourier_table.T, precision=lax.Precision.HIGHEST, preferred_element_type=jnp.float32) * (1.0 / math.sqrt(NF))
    return (adjoint_source, misfits.reshape(PAIRS))
```

```python
import functools
import math

import jax
import jax.numpy as jnp
from jax import lax
from jax.experimental import pallas as pl
from jax.experimental.pallas import tpu as pltpu
from jax.sharding import PartitionSpec as P

K0 = 64
CAP = 4
STEP = 64
MESH = pl.DeviceIdType.MESH
F32 = jnp.float32
BF16 = jnp.bfloat16


def iota(shape, axis):
    return lax.broadcasted_iota(jnp.int32, shape, axis)


def one_hot(mask):
    return jnp.where(mask, 1.0, 0.0).astype(BF16)


def dot(left, right):
    return jnp.dot(left, right, preferred_element_type=F32)


def dot_t(left, right):
    return lax.dot_general(left, right, (((1,), (1,)), ((), ())), preferred_element_type=F32)


def halves(value):
    high = value.astype(BF16)
    return high, (value - high.astype(F32)).astype(BF16)


def dot2(left, pair):
    return dot(left, pair[0]) + dot(left, pair[1])


def kernel(
    n,
    m,
    chunks,
    rec_ref,
    vs_ref,
    grow_ref,
    gcol_ref,
    prec_ref,
    psrc_ref,
    obs_ref,
    out_ref,
    mis_ref,
    obs_send,
    obs_recv,
    meta_send,
    meta_recv,
    src_send,
    src_mid,
    src_part,
    src_recv,
    adj_send,
    adj_recv,
    mis_send,
    mis_recv,
    table,
    cos_a,
    sin_a,
    cos_b,
    sin_b,
    spec,
    white_hi,
    white_lo,
    g1_ref,
    g2_ref,
    g1t_ref,
    g2t_ref,
    h_ref,
    mis_acc,
    send_sems,
    recv_sems,
    rs_send,
    rs_recv,
):
    chans, time_len = rec_ref.shape
    pairs, width = obs_ref.shape
    bins = width // 2
    part = bins // chunks
    rows_out = chans // m
    sources = vs_ref.shape[0]
    slots = n * CAP
    rows = 2 * slots
    me = lax.axis_index("chan")
    owner = lax.axis_index("src")
    META, SRC1, SRC2, MIS = chunks, chunks + 1, chunks + 2, chunks + 3

    barrier = pltpu.get_barrier_semaphore()

    def greet(i, carry):
        pl.semaphore_signal(
            barrier, inc=1, device_id={"chan": lax.rem(me + i, n)}, device_id_type=MESH
        )
        return carry

    lax.fori_loop(1, n, greet, 0)
    for i in range(1, m):
        pl.semaphore_signal(
            barrier, inc=1, device_id={"src": lax.rem(owner + i, m)}, device_id_type=MESH
        )

    def spread(send, recv, sem):
        def one(i, carry):
            other = lax.rem(me + i, n)
            pltpu.make_async_remote_copy(
                src_ref=send(other),
                dst_ref=recv.at[me],
                send_sem=send_sems.at[sem],
                recv_sem=recv_sems.at[sem],
                device_id={"chan": other},
                device_id_type=MESH,
            ).start()
            return carry

        pltpu.make_async_copy(send(me), recv.at[me], recv_sems.at[sem]).start()
        lax.fori_loop(1, n, one, 0)

    def arrived(recv, sem):
        pltpu.make_async_copy(recv, recv, recv_sems.at[sem]).wait()

    def left(recv, sem):
        some = recv.at[pl.ds(0, n - 1)]
        pltpu.make_async_copy(some, some, send_sems.at[sem]).wait()

    grow = grow_ref[...]
    before = (gcol_ref[...] == grow) & (iota((pairs, pairs), 0) < iota((pairs, pairs), 1))
    rank = jnp.sum(jnp.where(before, 1, 0), axis=0, keepdims=True)
    slot = grow * CAP + rank
    row_id = iota((rows, 2 * pairs), 0)
    row_slot = (row_id >> 3) * CAP + (row_id & 3)
    col_id = iota((rows, 2 * pairs), 1)
    imag_row = (row_id >> 2) & 1
    imag_col = jnp.where(col_id >= pairs, 1, 0)
    slot2 = jnp.concatenate([slot, slot], axis=1)
    place = one_hot((slot2 == row_slot) & (imag_row == imag_col))
    for q in range(chunks):
        lo, hi = q * part, (q + 1) * part
        block = jnp.concatenate(
            [obs_ref[:, lo:hi], obs_ref[:, bins + lo : bins + hi]], axis=0
        )
        obs_send[q] = dot2(place, halves(block)).reshape(n, 8, part)

    pick = slot == iota((slots, pairs), 0)
    slot_recv = jnp.sum(
        jnp.where(pick, prec_ref[...].astype(F32) + 1.0, 0.0), axis=1, keepdims=True
    )
    slot_src = jnp.sum(jnp.where(pick, psrc_ref[...].astype(F32), 0.0), axis=1, keepdims=True)
    lane = iota((slots, 128), 1)
    slot_rank = iota((slots, 128), 0) & 3
    coded = jnp.where(lane == slot_rank, slot_recv, 0.0) + jnp.where(
        lane == slot_rank + CAP, slot_src, 0.0
    )
    fold = one_hot(iota((n, slots), 0) == (iota((n, slots), 1) >> 2))
    meta_send[...] = dot(fold, coded.astype(BF16)).reshape(n, 1, 128)

    pl.semaphore_wait(barrier, n - 1 + m - 1)

    spread(lambda g: meta_send.at[g], meta_recv, META)
    for q in range(min(2, chunks)):
        spread(lambda g, q=q: obs_send.at[q, g], obs_recv.at[q], q)

    unit = math.pi / time_len
    steps = time_len // STEP
    bin_b = K0 + iota((STEP, bins), 1)
    phase_b = (bin_b * iota((STEP, bins), 0)) & (2 * time_len - 1)
    angle_b = phase_b.astype(F32) * unit
    cos_b[...] = jnp.cos(angle_b)
    sin_b[...] = jnp.sin(angle_b)
    phase_a = ((K0 + iota((steps, bins), 1)) * (iota((steps, bins), 0) * STEP)) & (2 * time_len - 1)
    angle_a = phase_a.astype(F32) * unit
    cos_a[...] = jnp.cos(angle_a).reshape(steps, 1, bins)
    sin_a[...] = jnp.sin(angle_a).reshape(steps, 1, bins)

    def fill(i, carry):
        ca, sa = cos_a[i], sin_a[i]
        cb, sb = cos_b[...], sin_b[...]
        at = pl.ds(pl.multiple_of(i * STEP, STEP), STEP)
        table[at, 0:bins] = (ca * cb - sa * sb).astype(BF16)
        table[at, bins : 2 * bins] = (-(sa * cb) - ca * sb).astype(BF16)
        return carry

    lax.fori_loop(0, steps, fill, 0)

    cols = min(256, width)

    def transform(i, power):
        at = pl.ds(pl.multiple_of(i * cols, cols), cols)
        values = dot(rec_ref[...], table[:, at])
        spec[:, at] = values
        return power + jnp.sum(values * values, axis=1, keepdims=True)

    power = lax.fori_loop(0, width // cols, transform, jnp.zeros((chans, 1), F32))
    norm = jnp.sqrt(power / bins + 1e-6)

    local = vs_ref[...] - me * chans
    chosen = one_hot(iota((sources, chans), 1) == local)
    for q in range(chunks):
        for h in range(2):
            at = slice(h * bins + q * part, h * bins + (q + 1) * part)
            high, low = halves(spec[:, at] / norm)
            for y in range(m):
                to = slice((2 * y + h) * rows_out, (2 * y + h + 1) * rows_out)
                white_hi[q, to, :] = high[y * rows_out : (y + 1) * rows_out, :]
                white_lo[q, to, :] = low[y * rows_out : (y + 1) * rows_out, :]
            picked = dot(chosen, high) + dot(chosen, low)
            for c in range(part // 128):
                block = (h * bins + q * part) // 128 + c
                for r in range(sources // 4):
                    src_send[r * (width // 128) + block] = picked[
                        4 * r : 4 * r + 4, 128 * c : 128 * (c + 1)
                    ]

    spread(lambda g: src_send.at[g], src_mid, SRC1)
    for q in range(2, min(3, chunks)):
        spread(lambda g, q=q: obs_send.at[q, g], obs_recv.at[q], q)
    arrived(src_mid, SRC1)
    src_part[...] = jnp.sum(src_mid[...], axis=0)
    spread(lambda g: src_part, src_recv, SRC2)
    for q in range(3, chunks):
        spread(lambda g, q=q: obs_send.at[q, g], obs_recv.at[q], q)

    arrived(meta_recv, META)
    unfold = one_hot((iota((rows, n), 0) >> 3) == iota((rows, n), 1))
    spread_meta = dot(unfold, meta_recv[...].reshape(n, 128).astype(BF16))
    lane = iota((rows, 128), 1)
    row_rank = iota((rows, 128), 0) & 3
    named = jnp.sum(jnp.where(lane == row_rank, spread_meta, 0.0), axis=1, keepdims=True)
    receiver = named.astype(jnp.int32) - 1
    source = jnp.sum(
        jnp.where(lane == row_rank + CAP, spread_meta, 0.0), axis=1, keepdims=True
    ).astype(jnp.int32)
    shift = rows_out.bit_length() - 1
    position = (receiver >> shift) * (2 * rows_out) + (receiver & (rows_out - 1))
    wide = (rows, 2 * chans)
    imag = (iota((rows, 1), 0) >> 2) & 1
    valid = receiver >= 0
    near = jnp.where(valid, position + imag * rows_out, -1)
    far = jnp.where(valid, position + (1 - imag) * rows_out, -1)
    sign = (1 - 2 * imag).astype(F32)
    g1 = jnp.where(iota(wide, 1) == near, 1.0, 0.0)
    g2 = jnp.where(iota(wide, 1) == far, sign, 0.0)
    g1_ref[...] = g1.astype(BF16)
    g2_ref[...] = g2.astype(BF16)
    g1t_ref[...] = g1.T.astype(BF16)
    g2t_ref[...] = g2.T.astype(BF16)
    h_ref[...] = one_hot((iota((rows, sources), 1) == source) & valid)

    arrived(src_recv, SRC2)

    def source_block(start):
        blocks = []
        for c in range(part // 128):
            block = start // 128 + c
            blocks.append(
                jnp.concatenate(
                    [src_recv[r * (width // 128) + block] for r in range(sources // 4)], axis=0
                )
            )
        return jnp.concatenate(blocks, axis=1)

    mis_acc[...] = jnp.zeros_like(mis_acc)

    def inverse(q):
        pltpu.make_async_copy(adj_recv.at[q], adj_recv.at[q], rs_recv.at[q]).wait()
        total = adj_recv[q, 0]
        for y in range(1, m):
            total = total + adj_recv[q, y]
        high, low = halves(total * (1.0 / math.sqrt(bins)))
        real = jnp.concatenate([high[:rows_out], low[:rows_out]], axis=0)
        imaginary = jnp.concatenate([high[rows_out:], low[rows_out:]], axis=0)
        span = min(512, time_len)

        def one(i, carry):
            at = pl.ds(pl.multiple_of(i * span, span), span)
            both = dot_t(real, table[at, q * part : (q + 1) * part]) + dot_t(
                imaginary, table[at, bins + q * part : bins + (q + 1) * part]
            )
            values = both[:rows_out] + both[rows_out:]
            if q == 0:
                out_ref[:, at] = values
            else:
                out_ref[:, at] += values
            return carry

        lax.fori_loop(0, time_len // span, one, 0)

    for q in range(chunks):
        arrived(obs_recv.at[q], q)
        band = (q * part + iota((1, part), 1)).astype(F32)
        taper = 0.5 - 0.5 * jnp.cos((band + 0.5) * (2.0 * math.pi / bins))
        s_re = dot2(h_ref[...], halves(source_block(q * part)))
        s_im = dot2(h_ref[...], halves(source_block(bins + q * part)))
        w_hi, w_lo = white_hi[q], white_lo[q]
        near_rows = dot2(g1_ref[...], (w_hi, w_lo))
        far_rows = dot2(g2_ref[...], (w_hi, w_lo))
        diff = s_re * near_rows + s_im * far_rows - obs_recv[q].reshape(rows, part)
        resid = taper * diff
        squares = resid * diff
        folded = squares[:, :128]
        for c in range(1, part // 128):
            folded = folded + squares[:, 128 * c : 128 * (c + 1)]
        mis_acc[...] += folded
        adj_send[q] = (
            dot2(g1t_ref[...], halves(resid * s_re)) + dot2(g2t_ref[...], halves(resid * s_im))
        ).reshape(m, 2 * rows_out, part)
        pltpu.make_async_copy(
            adj_send.at[q, owner], adj_recv.at[q, owner], rs_recv.at[q]
        ).start()
        for i in range(1, m):
            other = lax.rem(owner + i, m)
            pltpu.make_async_remote_copy(
                src_ref=adj_send.at[q, other],
                dst_ref=adj_recv.at[q, owner],
                send_sem=rs_send.at[q],
                recv_sem=rs_recv.at[q],
                device_id={"src": other},
                device_id_type=MESH,
            ).start()
        if q == chunks - 1:
            total = jnp.sum(mis_acc[...], axis=1, keepdims=True) * (0.5 / bins)
            spread_out = jnp.where(lane == row_rank, total, 0.0)
            fold8 = one_hot(iota((n, rows), 0) == (iota((n, rows), 1) >> 3))
            mis_send[...] = dot2(fold8, halves(spread_out)).reshape(n, 1, 128)
            spread(lambda g: mis_send.at[g], mis_recv, MIS)
        if q >= 1:
            inverse(q - 1)
    inverse(chunks - 1)

    arrived(mis_recv, MIS)
    unfold4 = one_hot((iota((slots, n), 0) >> 2) == iota((slots, n), 1))
    back = dot2(unfold4, halves(mis_recv[...].reshape(n, 128)))
    column = jnp.sum(
        jnp.where(iota((slots, 128), 1) == (iota((slots, 128), 0) & 3), back, 0.0),
        axis=1,
        keepdims=True,
    )
    mis_ref[...] = jnp.sum(jnp.where(pick, column, 0.0), axis=0, keepdims=True)

    for q in range(chunks):
        left(obs_recv.at[q], q)
        some = adj_recv.at[q, pl.ds(0, m - 1)]
        pltpu.make_async_copy(some, some, rs_send.at[q]).wait()
    left(meta_recv, META)
    left(src_mid, SRC1)
    left(src_recv, SRC2)
    left(mis_recv, MIS)


def per_device(n, m, records, virtual_sources, pair_group, pair_receiver, pair_source, observed):
    chans, time_len = records.shape
    pairs, width = observed.shape
    bins = width // 2
    chunks = max(1, bins // 256)
    part = bins // chunks
    rows_out = chans // m
    sources = virtual_sources.shape[0]
    rows = 2 * n * CAP
    group_row = pair_group.reshape(1, pairs)
    group_col = pair_group.reshape(pairs, 1)
    adjoint, misfit = pl.pallas_call(
        functools.partial(kernel, n, m, chunks),
        out_shape=(
            jax.ShapeDtypeStruct((rows_out, time_len), F32),
            jax.ShapeDtypeStruct((1, pairs), F32),
        ),
        in_specs=[pl.BlockSpec(memory_space=pltpu.VMEM)] * 7,
        out_specs=(pl.BlockSpec(memory_space=pltpu.VMEM),) * 2,
        scratch_shapes=[
            pltpu.VMEM((chunks, n, 8, part), F32),
            pltpu.VMEM((chunks, n, 8, part), F32),
            pltpu.VMEM((n, 1, 128), F32),
            pltpu.VMEM((n, 1, 128), F32),
            pltpu.VMEM((n, 4, 128), F32),
            pltpu.VMEM((n, 4, 128), F32),
            pltpu.VMEM((4, 128), F32),
            pltpu.VMEM((n, 4, 128), F32),
            pltpu.VMEM((chunks, m, 2 * rows_out, part), F32),
            pltpu.VMEM((chunks, m, 2 * rows_out, part), F32),
            pltpu.VMEM((n, 1, 128), F32),
            pltpu.VMEM((n, 1, 128), F32),
            pltpu.VMEM((time_len, width), BF16),
            pltpu.VMEM((time_len // STEP, 1, bins), F32),
            pltpu.VMEM((time_len // STEP, 1, bins), F32),
            pltpu.VMEM((STEP, bins), F32),
            pltpu.VMEM((STEP, bins), F32),
            pltpu.VMEM((chans, width), F32),
            pltpu.VMEM((chunks, 2 * chans, part), BF16),
            pltpu.VMEM((chunks, 2 * chans, part), BF16),
            pltpu.VMEM((rows, 2 * chans), BF16),
            pltpu.VMEM((rows, 2 * chans), BF16),
            pltpu.VMEM((2 * chans, rows), BF16),
            pltpu.VMEM((2 * chans, rows), BF16),
            pltpu.VMEM((rows, sources), BF16),
            pltpu.VMEM((rows, 128), F32),
            pltpu.SemaphoreType.DMA((chunks + 4,)),
            pltpu.SemaphoreType.DMA((chunks + 4,)),
            pltpu.SemaphoreType.DMA((chunks,)),
            pltpu.SemaphoreType.DMA((chunks,)),
        ],
        compiler_params=pltpu.CompilerParams(
            collective_id=0, has_side_effects=True, vmem_limit_bytes=56 * 1024 * 1024
        ),
    )(
        records,
        virtual_sources.reshape(sources, 1),
        group_row,
        group_col,
        pair_receiver.reshape(1, pairs),
        pair_source.reshape(1, pairs),
        observed,
    )
    return adjoint, misfit.reshape(pairs)


def solution(mesh):
    return jax.shard_map(
        functools.partial(per_device, mesh.shape["chan"], mesh.shape["src"]),
        mesh=mesh,
        in_specs=(
            P("chan", None),
            P("src"),
            P(("chan", "src"), None),
            P(("chan", "src")),
            P(("chan", "src")),
            P(("chan", "src"), None),
        ),
        out_specs=(P(("chan", "src"), None), P(("chan", "src"))),
        check_vma=False,
    )
```

```python
import functools
import math

import jax
import jax.numpy as jnp
from jax import lax
from jax.experimental import pallas as pl
from jax.experimental.pallas import tpu as pltpu
from jax.sharding import PartitionSpec as P

K0 = 64
CAP = 4
STEP = 64
PART = 128
MESH = pl.DeviceIdType.MESH
F32 = jnp.float32
BF16 = jnp.bfloat16


def iota(shape, axis):
    return lax.broadcasted_iota(jnp.int32, shape, axis)


def ones_where(mask):
    return jnp.where(mask, 1.0, 0.0)


def one_hot(mask):
    return ones_where(mask).astype(BF16)


def dot(left, right):
    return jnp.dot(left, right, preferred_element_type=F32)


def dot_t(left, right):
    return lax.dot_general(left, right, (((1,), (1,)), ((), ())), preferred_element_type=F32)


def halves(value):
    high = value.astype(BF16)
    return high, (value - high.astype(F32)).astype(BF16)


def dot2(left, pair):
    return dot(left, pair[0]) + dot(left, pair[1])


def lanes_of(values, lane):
    return jnp.sum(jnp.where(iota(values.shape, 1) == lane, values, 0.0), axis=1, keepdims=True)


def kernel(
    nz,
    np_,
    m,
    room,
    rec_ref,
    vs_ref,
    group_ref,
    prec_ref,
    psrc_ref,
    obs_ref,
    out_ref,
    mis_ref,
    over_ref,
    z_send,
    z_recv,
    x_send,
    x_recv,
    zmeta_send,
    zmeta_recv,
    xmeta_send,
    xmeta_recv,
    src_send,
    src_mid,
    src_part,
    src_line,
    src_all,
    src_recv,
    adj_send,
    adj_recv,
    xmis_send,
    xmis_recv,
    zmis_send,
    zmis_recv,
    flag_send,
    flag_recv,
    table,
    cos_a,
    sin_a,
    cos_b,
    sin_b,
    spec,
    white_hi,
    white_lo,
    perm_ref,
    g_ref,
    gt_ref,
    h_ref,
    mis_acc,
    zs_sem,
    zr_sem,
    xs_sem,
    xr_sem,
    ys_sem,
    yr_sem,
    small_s,
    small_r,
):
    chans, time_len = rec_ref.shape
    pairs, width = obs_ref.shape
    bins = width // 2
    chunks = bins // PART
    rows_out = chans // m
    sources = vs_ref.shape[1]
    z_rows = nz * room
    plane_slots = nz * CAP
    slots = np_ * plane_slots
    me = lax.axis_index("chan")
    owner = lax.axis_index("src")
    my_z = lax.rem(me // 2, nz)
    my_p = (me // (2 * nz)) * 2 + lax.rem(me, 2)

    def on_line(z):
        return {"chan": (me // (2 * nz)) * (2 * nz) + z * 2 + lax.rem(me, 2)}

    def in_plane(p):
        return {"chan": (p // 2) * (2 * nz) + my_z * 2 + lax.rem(p, 2)}

    def in_column(y):
        return {"src": y}

    barrier = pltpu.get_barrier_semaphore()

    def greet(size, mine, where):
        def one(i, carry):
            pl.semaphore_signal(
                barrier, inc=1, device_id=where(lax.rem(mine + i, size)), device_id_type=MESH
            )
            return carry

        lax.fori_loop(1, size, one, 0)

    greet(nz, my_z, on_line)
    greet(np_, my_p, in_plane)
    greet(m, owner, in_column)

    def spread(size, mine, where, send, recv, send_sem, recv_sem):
        def one(i, carry):
            other = lax.rem(mine + i, size)
            pltpu.make_async_remote_copy(
                src_ref=send(other),
                dst_ref=recv.at[mine],
                send_sem=send_sem,
                recv_sem=recv_sem,
                device_id=where(other),
                device_id_type=MESH,
            ).start()
            return carry

        pltpu.make_async_copy(send(mine), recv.at[mine], recv_sem).start()
        lax.fori_loop(1, size, one, 0)

    def arrived(recv, sem):
        pltpu.make_async_copy(recv, recv, sem).wait()

    def left(recv, sem):
        some = recv.at[pl.ds(0, recv.shape[0] - 1)]
        pltpu.make_async_copy(some, some, sem).wait()

    def spread_z(send, recv, send_sem, recv_sem):
        spread(nz, my_z, on_line, send, recv, send_sem, recv_sem)

    def spread_x(send, recv, send_sem, recv_sem):
        spread(np_, my_p, in_plane, send, recv, send_sem, recv_sem)

    ZMETA, XMETA, SRC1, SRC2, SRC3, XMIS, ZMIS, FLAG = range(8)

    diagonal = iota((pairs, pairs), 0) == iota((pairs, pairs), 1)
    earlier = iota((pairs, pairs), 0) < iota((pairs, pairs), 1)
    group = group_ref[...]
    group_col = jnp.sum(jnp.where(diagonal, group, 0), axis=1, keepdims=True)
    rank = jnp.sum(jnp.where((group_col == group) & earlier, 1, 0), axis=0, keepdims=True)
    slab = lax.rem(group >> 1, nz)
    slab_col = lax.rem(group_col >> 1, nz)
    place = jnp.sum(jnp.where((slab_col == slab) & earlier, 1, 0), axis=0, keepdims=True)
    plane = lax.div(group, 2 * nz) * 2 + (group & 1)
    over = jnp.max(jnp.where(place >= room, 1.0, 0.0), axis=1, keepdims=True)
    row = jnp.where(place < room, slab * room + place, -1)
    pick = ones_where(row == iota((z_rows, pairs), 0))
    pick_bf = pick.astype(BF16)

    def pack(q):
        block = jnp.concatenate(
            [
                obs_ref[:, q * PART : (q + 1) * PART],
                obs_ref[:, bins + q * PART : bins + (q + 1) * PART],
            ],
            axis=1,
        )
        values = dot2(pick_bf, halves(block))
        z_send[q, :, 0:room, :] = values[:, :PART].reshape(nz, room, PART)
        z_send[q, :, room : 2 * room, :] = values[:, PART:].reshape(nz, room, PART)

    def send_z(q):
        spread_z(lambda z: z_send.at[q, z], z_recv.at[q], zs_sem.at[q], zr_sem.at[q])

    pack(0)
    lane_z = iota((z_rows, 128), 1)
    rank_z = lax.rem(iota((z_rows, 128), 0), room)

    def along(values):
        return jnp.sum(jnp.where(pick > 0.5, values.astype(F32), 0.0), axis=1, keepdims=True)

    coded = (
        jnp.where(lane_z == rank_z, along(plane * CAP + rank + 1), 0.0)
        + jnp.where(lane_z == rank_z + 32, along(prec_ref[...]), 0.0)
        + jnp.where(lane_z == rank_z + 64, along(psrc_ref[...]), 0.0)
    )
    fold_z = one_hot(
        iota((nz, z_rows), 0) == lax.div(iota((nz, z_rows), 1), room)
    )
    zmeta = dot(fold_z, coded.astype(BF16)) + jnp.where(iota((nz, 128), 1) == 100, over, 0.0)
    zmeta_send[...] = zmeta.reshape(nz, 1, 128)

    pl.semaphore_wait(barrier, nz - 1 + np_ - 1 + m - 1)

    spread_z(lambda z: zmeta_send.at[z], zmeta_recv, small_s.at[ZMETA], small_r.at[ZMETA])
    send_z(0)
    first = min(4, chunks)
    for q in range(1, first):
        pack(q)
        send_z(q)
    for q in range(first, chunks):
        pack(q)

    unit = math.pi / time_len
    steps = time_len // STEP
    phase_b = ((K0 + iota((STEP, bins), 1)) * iota((STEP, bins), 0)) & (2 * time_len - 1)
    angle_b = phase_b.astype(F32) * unit
    cos_b[...] = jnp.cos(angle_b)
    sin_b[...] = jnp.sin(angle_b)
    phase_a = ((K0 + iota((steps, bins), 1)) * (iota((steps, bins), 0) * STEP)) & (2 * time_len - 1)
    angle_a = phase_a.astype(F32) * unit
    cos_a[...] = jnp.cos(angle_a).reshape(steps, 1, bins)
    sin_a[...] = jnp.sin(angle_a).reshape(steps, 1, bins)

    def fill(i, carry):
        at = pl.ds(pl.multiple_of(i * STEP, STEP), STEP)
        for q in range(chunks):
            part = slice(q * PART, (q + 1) * PART)
            ca, sa = cos_a[i, :, part], sin_a[i, :, part]
            cb, sb = cos_b[:, part], sin_b[:, part]
            table[at, 2 * q * PART : (2 * q + 1) * PART] = (ca * cb - sa * sb).astype(BF16)
            table[at, (2 * q + 1) * PART : (2 * q + 2) * PART] = (-(sa * cb) - ca * sb).astype(BF16)
        return carry

    lax.fori_loop(0, steps, fill, 0)

    def transform(i, power):
        at = pl.ds(pl.multiple_of(i * 2 * PART, 2 * PART), 2 * PART)
        values = dot(rec_ref[...], table[:, at])
        spec[:, at] = values
        return power + jnp.sum(values * values, axis=1, keepdims=True)

    power = lax.fori_loop(0, chunks, transform, jnp.zeros((chans, 1), F32))
    norm = jnp.sqrt(power / bins + 1e-6)

    wanted = jnp.sum(
        jnp.where(iota((sources, sources), 0) == iota((sources, sources), 1), vs_ref[...], 0),
        axis=1,
        keepdims=True,
    )
    chosen = one_hot(iota((sources, chans), 1) == wanted - me * chans)
    for q in range(chunks):
        pair = halves(spec[:, 2 * q * PART : (2 * q + 2) * PART] / norm)
        white_hi[q], white_lo[q] = pair
        src_send[q] = dot2(chosen, pair)
    spread_x(lambda p: src_send.at[p], src_mid, small_s.at[SRC1], small_r.at[SRC1])

    arrived(zmeta_recv, small_r.at[ZMETA])
    unfold_z = one_hot(lax.div(iota((z_rows, nz), 0), room) == iota((z_rows, nz), 1))
    metas = zmeta_recv[...].reshape(nz, 128)
    line_over = jnp.max(jnp.where(iota((nz, 128), 1) == 100, metas, 0.0), keepdims=True)
    wide = dot(unfold_z, metas.astype(BF16))
    code = lanes_of(wide, rank_z).astype(jnp.int32) - 1
    came_from = lax.div(iota((z_rows, 1), 0), room)
    to_plane = jnp.where(code >= 0, code >> 2, -1)
    within = came_from * CAP + (code & 3)
    target = jnp.where(code >= 0, to_plane * plane_slots + within, -1)
    perm_ref[...] = ones_where(iota((z_rows, slots), 1) == target).T.astype(BF16)
    to_plane_hot = ones_where(iota((z_rows, 128), 1) == to_plane)
    coded = jnp.where(lane_z == within, lanes_of(wide, rank_z + 32) + 1.0, 0.0) + jnp.where(
        lane_z == within + plane_slots, lanes_of(wide, rank_z + 64), 0.0
    )
    xmeta = dot(to_plane_hot.T[:np_].astype(BF16), coded.astype(BF16)) + jnp.where(
        iota((np_, 128), 1) == 100, line_over, 0.0
    )
    xmeta_send[...] = xmeta.reshape(np_, 1, 128)
    spread_x(lambda p: xmeta_send.at[p], xmeta_recv, small_s.at[XMETA], small_r.at[XMETA])

    def forward_x(q):
        arrived(z_recv.at[q], zr_sem.at[q])
        block = jnp.concatenate(
            [
                z_recv[q, :, 0:room, :].reshape(z_rows, PART),
                z_recv[q, :, room : 2 * room, :].reshape(z_rows, PART),
            ],
            axis=1,
        )
        values = dot2(perm_ref[...], halves(block))
        x_send[q, :, 0:plane_slots, :] = values[:, :PART].reshape(np_, plane_slots, PART)
        x_send[q, :, plane_slots : 2 * plane_slots, :] = values[:, PART:].reshape(
            np_, plane_slots, PART
        )
        spread_x(lambda p: x_send.at[q, p], x_recv.at[q], xs_sem.at[q], xr_sem.at[q])

    forward_x(0)

    arrived(src_mid, small_r.at[SRC1])
    src_part[...] = jnp.sum(src_mid[...], axis=0)
    spread_z(lambda z: src_part, src_line, small_s.at[SRC2], small_r.at[SRC2])
    second = min(6, chunks)
    for q in range(first, second):
        send_z(q)
    for q in range(1, first):
        forward_x(q)

    arrived(xmeta_recv, small_r.at[XMETA])
    unfold_x = one_hot(lax.div(iota((slots, np_), 0), plane_slots) == iota((slots, np_), 1))
    metas = xmeta_recv[...].reshape(np_, 128)
    flag_send[...] = jnp.broadcast_to(
        jnp.max(jnp.where(iota((np_, 128), 1) == 100, metas, 0.0), keepdims=True), (1, 128)
    )
    spread(m, owner, in_column, lambda y: flag_send, flag_recv, small_s.at[FLAG], small_r.at[FLAG])
    wide = dot(unfold_x, metas.astype(BF16))
    lane_x = lax.rem(iota((slots, 128), 0), plane_slots)
    receiver = lanes_of(wide, lane_x).astype(jnp.int32) - 1
    source = lanes_of(wide, lane_x + plane_slots).astype(jnp.int32)
    hits = ones_where(iota((slots, chans), 1) == receiver)
    g_ref[...] = hits.astype(BF16)
    gt_ref[...] = hits.T.astype(BF16)
    h_ref[...] = one_hot((iota((slots, sources), 1) == source) & (receiver >= 0))

    arrived(src_line, small_r.at[SRC2])
    src_all[...] = jnp.sum(src_line[...], axis=0)
    spread_x(lambda p: src_all, src_recv, small_s.at[SRC3], small_r.at[SRC3])
    for q in range(second, chunks):
        send_z(q)
    arrived(src_recv, small_r.at[SRC3])

    mis_acc[...] = jnp.zeros_like(mis_acc)

    def correlate(q):
        arrived(x_recv.at[q], xr_sem.at[q])
        band = (q * PART + iota((1, PART), 1)).astype(F32)
        taper = 0.5 - 0.5 * jnp.cos((band + 0.5) * (2.0 * math.pi / bins))
        source_rows = dot2(h_ref[...], halves(src_recv[q]))
        receiver_rows = dot2(g_ref[...], (white_hi[q], white_lo[q]))
        s_re, s_im = source_rows[:, :PART], source_rows[:, PART:]
        r_re, r_im = receiver_rows[:, :PART], receiver_rows[:, PART:]
        d_re = s_re * r_re + s_im * r_im - x_recv[q, :, 0:plane_slots, :].reshape(slots, PART)
        d_im = s_re * r_im - s_im * r_re - x_recv[q, :, plane_slots : 2 * plane_slots, :].reshape(
            slots, PART
        )
        e_re, e_im = taper * d_re, taper * d_im
        mis_acc[...] += e_re * d_re + e_im * d_im
        terms = jnp.concatenate([e_re * s_re - e_im * s_im, e_re * s_im + e_im * s_re], axis=1)
        adj_send[q] = dot2(gt_ref[...], halves(terms)).reshape(m, rows_out, 2 * PART)
        spread(
            m,
            owner,
            in_column,
            lambda y: adj_send.at[q, y],
            adj_recv.at[q],
            ys_sem.at[q],
            yr_sem.at[q],
        )

    def inverse(q):
        arrived(adj_recv.at[q], yr_sem.at[q])
        total = adj_recv[q, 0]
        for y in range(1, m):
            total = total + adj_recv[q, y]
        high, low = halves(total * (1.0 / math.sqrt(bins)))
        both = jnp.concatenate([high, low], axis=0)
        span = min(512, time_len)

        def one(i, carry):
            at = pl.ds(pl.multiple_of(i * span, span), span)
            product = dot_t(both, table[at, 2 * q * PART : (2 * q + 2) * PART])
            values = product[:rows_out] + product[rows_out:]
            if q == 0:
                out_ref[:, at] = values
            else:
                out_ref[:, at] += values
            return carry

        lax.fori_loop(0, time_len // span, one, 0)

    for q in range(chunks):
        correlate(q)
        if q + first < chunks:
            forward_x(q + first)
        if q >= 2 and q < chunks - 1:
            inverse(q - 2)

    total = jnp.sum(mis_acc[...], axis=1, keepdims=True) * (0.5 / bins)
    fold_x = one_hot(iota((np_, slots), 0) == lax.div(iota((np_, slots), 1), plane_slots))
    spread_out = jnp.where(iota((slots, 128), 1) == lane_x, total, 0.0)
    xmis_send[...] = dot2(fold_x, halves(spread_out)).reshape(np_, 1, 128)
    spread_x(lambda p: xmis_send.at[p], xmis_recv, small_s.at[XMIS], small_r.at[XMIS])

    for q in range(max(0, chunks - 3), chunks - 1):
        inverse(q)

    arrived(xmis_recv, small_r.at[XMIS])
    back = dot2(to_plane_hot[:, :np_].astype(BF16), halves(xmis_recv[...].reshape(np_, 128)))
    spread_out = jnp.where(lane_z == rank_z, lanes_of(back, within), 0.0)
    zmis_send[...] = dot2(fold_z, halves(spread_out)).reshape(nz, 1, 128)
    spread_z(lambda z: zmis_send.at[z], zmis_recv, small_s.at[ZMIS], small_r.at[ZMIS])

    inverse(chunks - 1)

    arrived(zmis_recv, small_r.at[ZMIS])
    back = dot2(unfold_z, halves(zmis_recv[...].reshape(nz, 128)))
    mis_ref[...] = jnp.sum(pick * lanes_of(back, rank_z), axis=0, keepdims=True)
    arrived(flag_recv, small_r.at[FLAG])
    over_ref[...] = jnp.max(flag_recv[...], axis=0)

    for q in range(chunks):
        left(z_recv.at[q], zs_sem.at[q])
        left(x_recv.at[q], xs_sem.at[q])
        left(adj_recv.at[q], ys_sem.at[q])
    for recv, sem in (
        (zmeta_recv, ZMETA),
        (xmeta_recv, XMETA),
        (src_mid, SRC1),
        (src_line, SRC2),
        (src_recv, SRC3),
        (xmis_recv, XMIS),
        (zmis_recv, ZMIS),
        (flag_recv, FLAG),
    ):
        left(recv, small_s.at[sem])


def exchange(nz, np_, m, room, number, operands):
    records, observed = operands[0], operands[5]
    chans, time_len = records.shape
    pairs, width = observed.shape
    bins = width // 2
    chunks = bins // PART
    rows_out = chans // m
    sources = operands[1].shape[1]
    slots = np_ * nz * CAP
    assert chunks == np_
    vmem = pltpu.VMEM
    return pl.pallas_call(
        functools.partial(kernel, nz, np_, m, room),
        out_shape=(
            jax.ShapeDtypeStruct((rows_out, time_len), F32),
            jax.ShapeDtypeStruct((1, pairs), F32),
            jax.ShapeDtypeStruct((1, 128), F32),
        ),
        in_specs=[pl.BlockSpec(memory_space=vmem)] * 6,
        out_specs=(pl.BlockSpec(memory_space=vmem),) * 3,
        scratch_shapes=[
            vmem((chunks, nz, 2 * room, PART), F32),
            vmem((chunks, nz, 2 * room, PART), F32),
            vmem((chunks, np_, 2 * nz * CAP, PART), F32),
            vmem((chunks, np_, 2 * nz * CAP, PART), F32),
            vmem((nz, 1, 128), F32),
            vmem((nz, 1, 128), F32),
            vmem((np_, 1, 128), F32),
            vmem((np_, 1, 128), F32),
            vmem((np_, sources, 2 * PART), F32),
            vmem((np_, sources, 2 * PART), F32),
            vmem((sources, 2 * PART), F32),
            vmem((nz, sources, 2 * PART), F32),
            vmem((sources, 2 * PART), F32),
            vmem((np_, sources, 2 * PART), F32),
            vmem((chunks, m, rows_out, 2 * PART), F32),
            vmem((chunks, m, rows_out, 2 * PART), F32),
            vmem((np_, 1, 128), F32),
            vmem((np_, 1, 128), F32),
            vmem((nz, 1, 128), F32),
            vmem((nz, 1, 128), F32),
            vmem((1, 128), F32),
            vmem((m, 1, 128), F32),
            vmem((time_len, width), BF16),
            vmem((time_len // STEP, 1, bins), F32),
            vmem((time_len // STEP, 1, bins), F32),
            vmem((STEP, bins), F32),
            vmem((STEP, bins), F32),
            vmem((chans, width), F32),
            vmem((chunks, chans, 2 * PART), BF16),
            vmem((chunks, chans, 2 * PART), BF16),
            vmem((slots, nz * room), BF16),
            vmem((slots, chans), BF16),
            vmem((chans, slots), BF16),
            vmem((slots, sources), BF16),
            vmem((slots, PART), F32),
            pltpu.SemaphoreType.DMA((chunks,)),
            pltpu.SemaphoreType.DMA((chunks,)),
            pltpu.SemaphoreType.DMA((chunks,)),
            pltpu.SemaphoreType.DMA((chunks,)),
            pltpu.SemaphoreType.DMA((chunks,)),
            pltpu.SemaphoreType.DMA((chunks,)),
            pltpu.SemaphoreType.DMA((8,)),
            pltpu.SemaphoreType.DMA((8,)),
        ],
        compiler_params=pltpu.CompilerParams(
            collective_id=number, has_side_effects=True, vmem_limit_bytes=56 * 1024 * 1024
        ),
    )(*operands)


def per_device(n, m, records, virtual_sources, pair_group, pair_receiver, pair_source, observed):
    pairs, width = observed.shape
    np_ = width // 2 // PART
    nz = n // np_
    most = np_ * CAP
    usual = max(8, most * 3 // 4 // 8 * 8)
    operands = (
        records,
        virtual_sources.reshape(1, -1),
        pair_group.reshape(1, pairs),
        pair_receiver.reshape(1, pairs),
        pair_source.reshape(1, pairs),
        observed,
    )
    adjoint, misfit, over = exchange(nz, np_, m, usual, 0, operands)
    adjoint, misfit = lax.cond(
        over[0, 0] > 0.0,
        lambda held: exchange(nz, np_, m, most, 1, operands)[:2],
        lambda held: held,
        (adjoint, misfit),
    )
    return adjoint, misfit.reshape(pairs)


def solution(mesh):
    return jax.shard_map(
        functools.partial(per_device, mesh.shape["chan"], mesh.shape["src"]),
        mesh=mesh,
        in_specs=(
            P("chan", None),
            P("src"),
            P(("chan", "src"), None),
            P(("chan", "src")),
            P(("chan", "src")),
            P(("chan", "src"), None),
        ),
        out_specs=(P(("chan", "src"), None), P(("chan", "src"))),
        check_vma=False,
    )
```

```python
import functools
import math

import jax
import jax.numpy as jnp
from jax import lax
from jax.experimental import pallas as pl
from jax.experimental.pallas import tpu as pltpu
from jax.sharding import PartitionSpec as P

K0 = 64
CAP = 4
STEP = 64
PART = 128
MESH = pl.DeviceIdType.MESH
F32 = jnp.float32
BF16 = jnp.bfloat16


def iota(shape, axis):
    return lax.broadcasted_iota(jnp.int32, shape, axis)


def ones_where(mask):
    return jnp.where(mask, 1.0, 0.0)


def one_hot(mask):
    return ones_where(mask).astype(BF16)


def dot(left, right):
    return jnp.dot(left, right, preferred_element_type=F32)


def dot_t(left, right):
    return lax.dot_general(left, right, (((1,), (1,)), ((), ())), preferred_element_type=F32)


def halves(value):
    high = value.astype(BF16)
    return high, (value - high.astype(F32)).astype(BF16)


def dot2(left, pair):
    return dot(left, pair[0]) + dot(left, pair[1])


def lanes_of(values, lane):
    return jnp.sum(jnp.where(iota(values.shape, 1) == lane, values, 0.0), axis=1, keepdims=True)


def kernel(
    nz,
    np_,
    m,
    room,
    rec_ref,
    vs_ref,
    group_ref,
    prec_ref,
    psrc_ref,
    obs_ref,
    out_ref,
    mis_ref,
    over_ref,
    z_send,
    z_recv,
    x_send,
    x_recv,
    zmeta_send,
    zmeta_recv,
    xmeta_send,
    xmeta_recv,
    src_send,
    src_mid,
    src_part,
    src_line,
    src_own,
    src_rows,
    src_all,
    src_recv,
    adj_send,
    adj_recv,
    mis_send,
    mis_recv,
    flag_send,
    flag_recv,
    tables,
    cos_a,
    sin_a,
    cos_b,
    sin_b,
    spec,
    white_hi,
    white_lo,
    perm_ref,
    g_ref,
    gt_ref,
    h_ref,
    mis_acc,
    zs_sem,
    zr_sem,
    xs_sem,
    xr_sem,
    ys_sem,
    yr_sem,
    small_s,
    small_r,
):
    chans, time_len = rec_ref.shape
    pairs, width = obs_ref.shape
    bins = width // 2
    chunks = bins // PART
    rows_out = chans // m
    sources = vs_ref.shape[1]
    z_rows = nz * room
    plane_slots = nz * CAP
    slots = np_ * plane_slots
    me = lax.axis_index("chan")
    owner = lax.axis_index("src")
    my_z = lax.rem(lax.div(me, 2), nz)
    my_p = lax.div(me, 2 * nz) * 2 + lax.rem(me, 2)
    line = [lax.rem(my_z + i, nz) for i in range(nz)]
    plane_ids = [lax.rem(my_p + i, np_) for i in range(np_)]
    owners = [lax.rem(owner + i, m) for i in range(m)]
    base = [lax.div(p, 2) * (2 * nz) + lax.rem(p, 2) for p in plane_ids]

    def there(i, j):
        return {"chan": base[i] + 2 * line[j]}

    on_line = [there(0, j) for j in range(nz)]
    in_plane = [there(i, 0) for i in range(np_)]
    in_column = [{"src": y} for y in owners]

    barrier = pltpu.get_barrier_semaphore()
    for devices in (on_line, in_plane, in_column):
        for device in devices[1:]:
            pl.semaphore_signal(barrier, inc=1, device_id=device, device_id_type=MESH)

    def spread(places, devices, send, recv, send_sem, recv_sem):
        mine = places[0]
        for place, device in zip(places[1:], devices[1:]):
            pltpu.make_async_remote_copy(
                src_ref=send(place),
                dst_ref=recv.at[mine],
                send_sem=send_sem,
                recv_sem=recv_sem,
                device_id=device,
                device_id_type=MESH,
            ).start()
        pltpu.make_async_copy(send(mine), recv.at[mine], recv_sem).start()

    def arrived(recv, sem):
        pltpu.make_async_copy(recv, recv, sem).wait()

    def left(recv, sem):
        some = recv.at[pl.ds(0, recv.shape[0] - 1)]
        pltpu.make_async_copy(some, some, sem).wait()

    def spread_z(send, recv, send_sem, recv_sem):
        spread(line, on_line, send, recv, send_sem, recv_sem)

    def spread_x(send, recv, send_sem, recv_sem):
        spread(plane_ids, in_plane, send, recv, send_sem, recv_sem)

    ZMETA, XMETA, SRC1, SRC2, SRC3, SRC4, MIS, FLAG = range(8)

    diagonal = iota((pairs, pairs), 0) == iota((pairs, pairs), 1)
    earlier = iota((pairs, pairs), 0) < iota((pairs, pairs), 1)
    group = group_ref[...]
    group_col = jnp.sum(jnp.where(diagonal, group, 0), axis=1, keepdims=True)
    rank = jnp.sum(jnp.where((group_col == group) & earlier, 1, 0), axis=0, keepdims=True)
    slab = lax.rem(group >> 1, nz)
    slab_col = lax.rem(group_col >> 1, nz)
    place = jnp.sum(jnp.where((slab_col == slab) & earlier, 1, 0), axis=0, keepdims=True)
    plane = lax.div(group, 2 * nz) * 2 + (group & 1)
    over = jnp.max(jnp.where(place >= room, 1.0, 0.0), axis=1, keepdims=True)
    row = jnp.where(place < room, slab * room + place, -1)
    pick = ones_where(row == iota((z_rows, pairs), 0))
    pick_bf = pick.astype(BF16)

    def pack(q):
        block = jnp.concatenate(
            [
                obs_ref[:, q * PART : (q + 1) * PART],
                obs_ref[:, bins + q * PART : bins + (q + 1) * PART],
            ],
            axis=1,
        )
        values = dot2(pick_bf, halves(block))
        z_send[q, :, 0:room, :] = values[:, :PART].reshape(nz, room, PART)
        z_send[q, :, room : 2 * room, :] = values[:, PART:].reshape(nz, room, PART)

    def send_z(q):
        spread_z(lambda z: z_send.at[q, z], z_recv.at[q], zs_sem.at[q], zr_sem.at[q])

    pack(0)
    lane_z = iota((z_rows, 128), 1)
    rank_z = lax.rem(iota((z_rows, 128), 0), room)

    def along(values):
        return jnp.sum(jnp.where(pick > 0.5, values.astype(F32), 0.0), axis=1, keepdims=True)

    coded = (
        jnp.where(lane_z == rank_z, along(plane * CAP + rank + 1), 0.0)
        + jnp.where(lane_z == rank_z + 32, along(prec_ref[...]), 0.0)
        + jnp.where(lane_z == rank_z + 64, along(psrc_ref[...]), 0.0)
    )
    fold_z = one_hot(
        iota((nz, z_rows), 0) == lax.div(iota((nz, z_rows), 1), room)
    )
    zmeta = dot(fold_z, coded.astype(BF16)) + jnp.where(iota((nz, 128), 1) == 100, over, 0.0)
    zmeta_send[...] = zmeta.reshape(nz, 1, 128)

    unit = math.pi / time_len
    steps = time_len // STEP
    phase_b = ((K0 + iota((STEP, bins), 1)) * iota((STEP, bins), 0)) & (2 * time_len - 1)
    angle_b = phase_b.astype(F32) * unit
    cos_b[...] = jnp.cos(angle_b)
    sin_b[...] = -jnp.sin(angle_b)
    phase_a = ((K0 + iota((steps, bins), 1)) * (iota((steps, bins), 0) * STEP)) & (2 * time_len - 1)
    angle_a = phase_a.astype(F32) * unit
    cos_a[...] = jnp.cos(angle_a).reshape(steps, 1, bins)
    sin_a[...] = -jnp.sin(angle_a).reshape(steps, 1, bins)

    span = 512
    power = jnp.zeros((chans, 1), F32)
    for q in range(chunks + 1):

        def step(i, total, q=q):
            at = pl.ds(pl.multiple_of(i * span, span), span)
            if q > 0:
                total = total + dot(rec_ref[:, at], tables[q - 1][at, :])
            if q < chunks:
                part = slice(q * PART, (q + 1) * PART)
                cb, sb = cos_b[:, part], sin_b[:, part]
                for b in range(span // STEP):
                    rows = pl.ds(pl.multiple_of(i * span + b * STEP, STEP), STEP)
                    ca = cos_a[i * (span // STEP) + b, :, part]
                    sa = sin_a[i * (span // STEP) + b, :, part]
                    tables[q][rows, 0:PART] = (ca * cb - sa * sb).astype(BF16)
                    tables[q][rows, PART : 2 * PART] = (sa * cb + ca * sb).astype(BF16)
            return total

        values = lax.fori_loop(
            0, time_len // span, step, jnp.zeros((chans, 2 * PART), F32)
        )
        if q > 0:
            spec[:, 2 * (q - 1) * PART : 2 * q * PART] = values
            power = power + jnp.sum(values * values, axis=1, keepdims=True)
    norm = jnp.sqrt(power / bins + 1e-6)

    wanted = jnp.sum(
        jnp.where(iota((sources, sources), 0) == iota((sources, sources), 1), vs_ref[...], 0),
        axis=1,
        keepdims=True,
    )
    chosen = one_hot(iota((sources, chans), 1) == wanted - me * chans)
    for q in range(chunks):
        pair = halves(spec[:, 2 * q * PART : (2 * q + 2) * PART] / norm)
        white_hi[q], white_lo[q] = pair
        src_send[q] = dot2(chosen, pair)

    pl.semaphore_wait(barrier, nz - 1 + np_ - 1 + m - 1)

    spread_x(lambda p: src_send.at[p], src_mid, small_s.at[SRC1], small_r.at[SRC1])
    spread_z(lambda z: zmeta_send.at[z], zmeta_recv, small_s.at[ZMETA], small_r.at[ZMETA])
    send_z(0)
    for q in range(1, chunks):
        pack(q)

    def forward_x(q):
        arrived(z_recv.at[q], zr_sem.at[q])
        block = jnp.concatenate(
            [
                z_recv[q, :, 0:room, :].reshape(z_rows, PART),
                z_recv[q, :, room : 2 * room, :].reshape(z_rows, PART),
            ],
            axis=1,
        )
        values = dot2(perm_ref[...], halves(block))
        x_send[q, :, 0:plane_slots, :] = values[:, :PART].reshape(np_, plane_slots, PART)
        x_send[q, :, plane_slots : 2 * plane_slots, :] = values[:, PART:].reshape(
            np_, plane_slots, PART
        )
        spread_x(lambda p: x_send.at[q, p], x_recv.at[q], xs_sem.at[q], xr_sem.at[q])

    def name_slots():
        arrived(xmeta_recv, small_r.at[XMETA])
        unfold_x = one_hot(lax.div(iota((slots, np_), 0), plane_slots) == iota((slots, np_), 1))
        metas = xmeta_recv[...].reshape(np_, 128)
        flag_send[...] = jnp.broadcast_to(
            jnp.max(jnp.where(iota((np_, 128), 1) == 100, metas, 0.0), keepdims=True), (1, 128)
        )
        spread(owners, in_column, lambda y: flag_send, flag_recv, small_s.at[FLAG], small_r.at[FLAG])
        wide = dot(unfold_x, metas.astype(BF16))
        lane_x = lax.rem(iota((slots, 128), 0), plane_slots)
        receiver = lanes_of(wide, lane_x).astype(jnp.int32) - 1
        source = lanes_of(wide, lane_x + plane_slots).astype(jnp.int32)
        hits = ones_where(iota((slots, chans), 1) == receiver)
        g_ref[...] = hits.astype(BF16)
        gt_ref[...] = hits.T.astype(BF16)
        h_ref[...] = one_hot((iota((slots, sources), 1) == source) & (receiver >= 0))

    arrived(src_mid, small_r.at[SRC1])
    part = jnp.sum(src_mid[...], axis=0)
    few = sources // nz
    for z in range(nz):
        src_part[z] = part[z * few : (z + 1) * few]
    spread_z(lambda z: src_part.at[z], src_line, small_s.at[SRC2], small_r.at[SRC2])
    send_z(1)

    arrived(zmeta_recv, small_r.at[ZMETA])
    unfold_z = one_hot(lax.div(iota((z_rows, nz), 0), room) == iota((z_rows, nz), 1))
    metas = zmeta_recv[...].reshape(nz, 128)
    line_over = jnp.max(jnp.where(iota((nz, 128), 1) == 100, metas, 0.0), keepdims=True)
    wide = dot(unfold_z, metas.astype(BF16))
    code = lanes_of(wide, rank_z).astype(jnp.int32) - 1
    came_from = lax.div(iota((z_rows, 1), 0), room)
    to_plane = jnp.where(code >= 0, code >> 2, -1)
    within = came_from * CAP + (code & 3)
    target = jnp.where(code >= 0, to_plane * plane_slots + within, -1)
    perm_ref[...] = ones_where(iota((z_rows, slots), 1) == target).T.astype(BF16)
    to_plane_hot = ones_where(iota((z_rows, 128), 1) == to_plane)
    coded = jnp.where(lane_z == within, lanes_of(wide, rank_z + 32) + 1.0, 0.0) + jnp.where(
        lane_z == within + plane_slots, lanes_of(wide, rank_z + 64), 0.0
    )
    xmeta = dot(to_plane_hot.T[:np_].astype(BF16), coded.astype(BF16)) + jnp.where(
        iota((np_, 128), 1) == 100, line_over, 0.0
    )
    xmeta_send[...] = xmeta.reshape(np_, 1, 128)
    spread_x(lambda p: xmeta_send.at[p], xmeta_recv, small_s.at[XMETA], small_r.at[XMETA])

    arrived(src_line, small_r.at[SRC2])
    src_own[...] = jnp.sum(src_line[...], axis=0)
    spread_z(lambda z: src_own, src_rows, small_s.at[SRC3], small_r.at[SRC3])
    send_z(2)
    forward_x(0)
    name_slots()
    arrived(src_rows, small_r.at[SRC3])
    src_all[...] = jnp.concatenate([src_rows[z] for z in range(nz)], axis=0)
    spread_x(lambda p: src_all, src_recv, small_s.at[SRC4], small_r.at[SRC4])
    send_z(3)
    forward_x(1)
    if chunks > 4:
        send_z(4)
    arrived(src_recv, small_r.at[SRC4])

    mis_acc[...] = jnp.zeros_like(mis_acc)

    def correlate(q):
        arrived(x_recv.at[q], xr_sem.at[q])
        band = (q * PART + iota((1, PART), 1)).astype(F32)
        taper = 0.5 - 0.5 * jnp.cos((band + 0.5) * (2.0 * math.pi / bins))
        source_rows = dot2(h_ref[...], halves(src_recv[q]))
        receiver_rows = dot2(g_ref[...], (white_hi[q], white_lo[q]))
        s_re, s_im = source_rows[:, :PART], source_rows[:, PART:]
        r_re, r_im = receiver_rows[:, :PART], receiver_rows[:, PART:]
        d_re = s_re * r_re + s_im * r_im - x_recv[q, :, 0:plane_slots, :].reshape(slots, PART)
        d_im = s_re * r_im - s_im * r_re - x_recv[q, :, plane_slots : 2 * plane_slots, :].reshape(
            slots, PART
        )
        e_re, e_im = taper * d_re, taper * d_im
        mis_acc[...] += e_re * d_re + e_im * d_im
        terms = jnp.concatenate([e_re * s_re - e_im * s_im, e_re * s_im + e_im * s_re], axis=1)
        adj_send[q] = dot2(gt_ref[...], halves(terms)).reshape(m, rows_out, 2 * PART)
        spread(
            owners,
            in_column,
            lambda y: adj_send.at[q, y],
            adj_recv.at[q],
            ys_sem.at[q],
            yr_sem.at[q],
        )

    def inverse(q):
        arrived(adj_recv.at[q], yr_sem.at[q])
        total = adj_recv[q, 0]
        for y in range(1, m):
            total = total + adj_recv[q, y]
        high, low = halves(total * (1.0 / math.sqrt(bins)))
        both = jnp.concatenate([high, low], axis=0)
        span = min(512, time_len)

        def one(i, carry):
            at = pl.ds(pl.multiple_of(i * span, span), span)
            product = dot_t(both, tables[q][at, :])
            values = product[:rows_out] + product[rows_out:]
            if q == 0:
                out_ref[:, at] = values
            else:
                out_ref[:, at] += values
            return carry

        lax.fori_loop(0, time_len // span, one, 0)

    for q in range(chunks):
        correlate(q)
        if q + 5 < chunks:
            send_z(q + 5)
        if q + 2 < chunks:
            forward_x(q + 2)
        if 2 <= q < chunks - 1:
            inverse(q - 2)

    lane_4 = iota((slots, 128), 0) & 3
    total = jnp.sum(mis_acc[...], axis=1, keepdims=True) * (0.5 / bins)
    count = nz * np_
    fold_4 = one_hot(iota((count, slots), 0) == (iota((count, slots), 1) >> 2))
    spread_out = jnp.where(iota((slots, 128), 1) == lane_4, total, 0.0)
    mis_send[...] = dot2(fold_4, halves(spread_out)).reshape(count, 1, 128)

    spread(
        [plane_ids[i] * nz + line[j] for i in range(np_) for j in range(nz)],
        [there(i, j) for i in range(np_) for j in range(nz)],
        lambda u: mis_send.at[u],
        mis_recv,
        small_s.at[MIS],
        small_r.at[MIS],
    )
    for q in range(max(0, chunks - 3), chunks):
        inverse(q)

    arrived(mis_recv, small_r.at[MIS])
    unfold_4 = one_hot((iota((slots, count), 0) >> 2) == iota((slots, count), 1))
    back = dot2(unfold_4, halves(mis_recv[...].reshape(count, 128)))
    own = ones_where((plane * nz + slab) * CAP + rank == iota((slots, pairs), 0))
    mis_ref[...] = jnp.sum(own * lanes_of(back, lane_4), axis=0, keepdims=True)
    arrived(flag_recv, small_r.at[FLAG])
    over_ref[...] = jnp.max(flag_recv[...], axis=0)

    for q in range(chunks):
        left(z_recv.at[q], zs_sem.at[q])
        left(x_recv.at[q], xs_sem.at[q])
        left(adj_recv.at[q], ys_sem.at[q])
    for recv, sem in (
        (zmeta_recv, ZMETA),
        (xmeta_recv, XMETA),
        (src_mid, SRC1),
        (src_line, SRC2),
        (src_rows, SRC3),
        (src_recv, SRC4),
        (mis_recv, MIS),
        (flag_recv, FLAG),
    ):
        left(recv, small_s.at[sem])


def exchange(nz, np_, m, room, number, operands):
    records, observed = operands[0], operands[5]
    chans, time_len = records.shape
    pairs, width = observed.shape
    bins = width // 2
    chunks = bins // PART
    rows_out = chans // m
    sources = operands[1].shape[1]
    slots = np_ * nz * CAP
    assert chunks == np_
    vmem = pltpu.VMEM
    return pl.pallas_call(
        functools.partial(kernel, nz, np_, m, room),
        out_shape=(
            jax.ShapeDtypeStruct((rows_out, time_len), F32),
            jax.ShapeDtypeStruct((1, pairs), F32),
            jax.ShapeDtypeStruct((1, 128), F32),
        ),
        in_specs=[pl.BlockSpec(memory_space=vmem)] * 6,
        out_specs=(pl.BlockSpec(memory_space=vmem),) * 3,
        scratch_shapes=[
            vmem((chunks, nz, 2 * room, PART), F32),
            vmem((chunks, nz, 2 * room, PART), F32),
            vmem((chunks, np_, 2 * nz * CAP, PART), F32),
            vmem((chunks, np_, 2 * nz * CAP, PART), F32),
            vmem((nz, 1, 128), F32),
            vmem((nz, 1, 128), F32),
            vmem((np_, 1, 128), F32),
            vmem((np_, 1, 128), F32),
            vmem((np_, sources, 2 * PART), F32),
            vmem((np_, sources, 2 * PART), F32),
            vmem((nz, sources // nz, 2 * PART), F32),
            vmem((nz, sources // nz, 2 * PART), F32),
            vmem((sources // nz, 2 * PART), F32),
            vmem((nz, sources // nz, 2 * PART), F32),
            vmem((sources, 2 * PART), F32),
            vmem((np_, sources, 2 * PART), F32),
            vmem((chunks, m, rows_out, 2 * PART), F32),
            vmem((chunks, m, rows_out, 2 * PART), F32),
            vmem((nz * np_, 1, 128), F32),
            vmem((nz * np_, 1, 128), F32),
            vmem((1, 128), F32),
            vmem((m, 1, 128), F32),
            [vmem((time_len, 2 * PART), BF16) for _ in range(chunks)],
            vmem((time_len // STEP, 1, bins), F32),
            vmem((time_len // STEP, 1, bins), F32),
            vmem((STEP, bins), F32),
            vmem((STEP, bins), F32),
            vmem((chans, width), F32),
            vmem((chunks, chans, 2 * PART), BF16),
            vmem((chunks, chans, 2 * PART), BF16),
            vmem((slots, nz * room), BF16),
            vmem((slots, chans), BF16),
            vmem((chans, slots), BF16),
            vmem((slots, sources), BF16),
            vmem((slots, PART), F32),
            pltpu.SemaphoreType.DMA((chunks,)),
            pltpu.SemaphoreType.DMA((chunks,)),
            pltpu.SemaphoreType.DMA((chunks,)),
            pltpu.SemaphoreType.DMA((chunks,)),
            pltpu.SemaphoreType.DMA((chunks,)),
            pltpu.SemaphoreType.DMA((chunks,)),
            pltpu.SemaphoreType.DMA((8,)),
            pltpu.SemaphoreType.DMA((8,)),
        ],
        compiler_params=pltpu.CompilerParams(
            collective_id=number, has_side_effects=True, vmem_limit_bytes=56 * 1024 * 1024
        ),
    )(*operands)


def per_device(n, m, records, virtual_sources, pair_group, pair_receiver, pair_source, observed):
    pairs, width = observed.shape
    np_ = width // 2 // PART
    nz = n // np_
    most = np_ * CAP
    usual = max(8, most * 3 // 4 // 8 * 8)
    operands = (
        records,
        virtual_sources.reshape(1, -1),
        pair_group.reshape(1, pairs),
        pair_receiver.reshape(1, pairs),
        pair_source.reshape(1, pairs),
        observed,
    )
    adjoint, misfit, over = exchange(nz, np_, m, usual, 0, operands)
    adjoint, misfit = lax.cond(
        over[0, 0] > 0.0,
        lambda held: exchange(nz, np_, m, most, 1, operands)[:2],
        lambda held: held,
        (adjoint, misfit),
    )
    return adjoint, misfit.reshape(pairs)


def solution(mesh):
    return jax.shard_map(
        functools.partial(per_device, mesh.shape["chan"], mesh.shape["src"]),
        mesh=mesh,
        in_specs=(
            P("chan", None),
            P("src"),
            P(("chan", "src"), None),
            P(("chan", "src")),
            P(("chan", "src")),
            P(("chan", "src"), None),
        ),
        out_specs=(P(("chan", "src"), None), P(("chan", "src"))),
        check_vma=False,
    )
```

```python
import functools
import math

import jax
import jax.numpy as jnp
from jax import lax
from jax.experimental import pallas as pl
from jax.experimental.pallas import tpu as pltpu
from jax.sharding import PartitionSpec as P

K0 = 64
CAP = 4
STEP = 64
PART = 128
MESH = pl.DeviceIdType.MESH
F32 = jnp.float32
BF16 = jnp.bfloat16


def iota(shape, axis):
    return lax.broadcasted_iota(jnp.int32, shape, axis)


def ones_where(mask):
    return jnp.where(mask, 1.0, 0.0)


def one_hot(mask):
    return ones_where(mask).astype(BF16)


def dot(left, right):
    return jnp.dot(left, right, preferred_element_type=F32)


def dot_t(left, right):
    return lax.dot_general(left, right, (((1,), (1,)), ((), ())), preferred_element_type=F32)


def halves(value):
    high = value.astype(BF16)
    return high, (value - high.astype(F32)).astype(BF16)


def dot2(left, pair):
    return dot(left, pair[0]) + dot(left, pair[1])


def lanes_of(values, lane):
    return jnp.sum(jnp.where(iota(values.shape, 1) == lane, values, 0.0), axis=1, keepdims=True)


def kernel(
    nz,
    np_,
    m,
    room,
    rec_ref,
    vs_ref,
    group_ref,
    prec_ref,
    psrc_ref,
    obs_ref,
    out_ref,
    mis_ref,
    over_ref,
    z_send,
    z_recv,
    x_send,
    x_recv,
    zmeta_send,
    zmeta_recv,
    xmeta_send,
    xmeta_recv,
    src_send,
    src_mid,
    src_part,
    src_line,
    src_own,
    src_rows,
    src_all,
    src_recv,
    adj_send,
    adj_recv,
    mis_send,
    mis_recv,
    flag_send,
    flag_recv,
    rec_halves,
    tables,
    cos_a,
    sin_a,
    cos_b,
    sin_b,
    spec,
    white,
    perm_ref,
    g_ref,
    gt_ref,
    h_ref,
    mis_acc,
    zs_sem,
    zr_sem,
    xs_sem,
    xr_sem,
    ys_sem,
    yr_sem,
    small_s,
    small_r,
):
    chans, time_len = rec_ref.shape
    pairs, width = obs_ref.shape
    bins = width // 2
    chunks = bins // PART
    rows_out = chans // m
    sources = vs_ref.shape[1]
    z_rows = nz * room
    plane_slots = nz * CAP
    slots = np_ * plane_slots
    me = lax.axis_index("chan")
    owner = lax.axis_index("src")
    my_z = lax.rem(lax.div(me, 2), nz)
    my_p = lax.div(me, 2 * nz) * 2 + lax.rem(me, 2)
    line = [lax.rem(my_z + i, nz) for i in range(nz)]
    plane_ids = [lax.rem(my_p + i, np_) for i in range(np_)]
    owners = [lax.rem(owner + i, m) for i in range(m)]
    base = [lax.div(p, 2) * (2 * nz) + lax.rem(p, 2) for p in plane_ids]

    def there(i, j):
        return {"chan": base[i] + 2 * line[j]}

    on_line = [there(0, j) for j in range(nz)]
    in_plane = [there(i, 0) for i in range(np_)]
    in_column = [{"src": y} for y in owners]

    barrier = pltpu.get_barrier_semaphore()
    for devices in (on_line, in_plane, in_column):
        for device in devices[1:]:
            pl.semaphore_signal(barrier, inc=1, device_id=device, device_id_type=MESH)

    def spread(places, devices, send, recv, send_sem, recv_sem):
        mine = places[0]
        for place, device in zip(places[1:], devices[1:]):
            pltpu.make_async_remote_copy(
                src_ref=send(place),
                dst_ref=recv.at[mine],
                send_sem=send_sem,
                recv_sem=recv_sem,
                device_id=device,
                device_id_type=MESH,
            ).start()
        pltpu.make_async_copy(send(mine), recv.at[mine], recv_sem).start()

    def arrived(recv, sem):
        pltpu.make_async_copy(recv, recv, sem).wait()

    def left(recv, sem):
        some = recv.at[pl.ds(0, recv.shape[0] - 1)]
        pltpu.make_async_copy(some, some, sem).wait()

    def spread_z(send, recv, send_sem, recv_sem):
        spread(line, on_line, send, recv, send_sem, recv_sem)

    def spread_x(send, recv, send_sem, recv_sem):
        spread(plane_ids, in_plane, send, recv, send_sem, recv_sem)

    ZMETA, XMETA, SRC1, SRC2, SRC3, SRC4, MIS, FLAG = range(8)

    diagonal = iota((pairs, pairs), 0) == iota((pairs, pairs), 1)
    earlier = iota((pairs, pairs), 0) < iota((pairs, pairs), 1)
    group = group_ref[...]
    group_col = jnp.sum(jnp.where(diagonal, group, 0), axis=1, keepdims=True)
    rank = jnp.sum(jnp.where((group_col == group) & earlier, 1, 0), axis=0, keepdims=True)
    slab = lax.rem(group >> 1, nz)
    slab_col = lax.rem(group_col >> 1, nz)
    place = jnp.sum(jnp.where((slab_col == slab) & earlier, 1, 0), axis=0, keepdims=True)
    plane = lax.div(group, 2 * nz) * 2 + (group & 1)
    over = jnp.max(jnp.where(place >= room, 1.0, 0.0), axis=1, keepdims=True)
    row = jnp.where(place < room, slab * room + place, -1)
    pick = ones_where(row == iota((z_rows, pairs), 0))
    pick_bf = jnp.concatenate([pick, pick], axis=1).astype(BF16)

    def pack(q):
        block = jnp.concatenate(
            [
                obs_ref[:, q * PART : (q + 1) * PART],
                obs_ref[:, bins + q * PART : bins + (q + 1) * PART],
            ],
            axis=1,
        )
        values = dot(pick_bf, jnp.concatenate(halves(block), axis=0))
        z_send[q, :, 0:room, :] = values[:, :PART].reshape(nz, room, PART)
        z_send[q, :, room : 2 * room, :] = values[:, PART:].reshape(nz, room, PART)

    def send_z(q):
        spread_z(lambda z: z_send.at[q, z], z_recv.at[q], zs_sem.at[q], zr_sem.at[q])

    pack(0)
    lane_z = iota((z_rows, 128), 1)
    rank_z = lax.rem(iota((z_rows, 128), 0), room)

    def along(values):
        return jnp.sum(jnp.where(pick > 0.5, values.astype(F32), 0.0), axis=1, keepdims=True)

    coded = (
        jnp.where(lane_z == rank_z, along(plane * CAP + rank + 1), 0.0)
        + jnp.where(lane_z == rank_z + 32, along(prec_ref[...]), 0.0)
        + jnp.where(lane_z == rank_z + 64, along(psrc_ref[...]), 0.0)
    )
    fold_z = one_hot(
        iota((nz, z_rows), 0) == lax.div(iota((nz, z_rows), 1), room)
    )
    zmeta = dot(fold_z, coded.astype(BF16)) + jnp.where(iota((nz, 128), 1) == 100, over, 0.0)
    zmeta_send[...] = zmeta.reshape(nz, 1, 128)

    half = time_len // 2
    steps = half // STEP
    digit = iota((32, bins), 0) >> 3
    times = (iota((32, bins), 0) & 7) * jnp.where(
        digit == 0, 1, jnp.where(digit == 1, 8, jnp.where(digit == 2, 64, 512))
    )
    phase = ((K0 + iota((32, bins), 1)) * times) & (2 * time_len - 1)
    angle = phase.astype(F32) * (math.pi / time_len)
    cos_d, sin_d = jnp.cos(angle), -jnp.sin(angle)
    for j in range(8):
        cj, sj = cos_d[8 + j : 9 + j], sin_d[8 + j : 9 + j]
        cos_b[8 * j : 8 * j + 8, :] = cj * cos_d[:8] - sj * sin_d[:8]
        sin_b[8 * j : 8 * j + 8, :] = sj * cos_d[:8] + cj * sin_d[:8]
    for j in range(steps // 8):
        cj, sj = cos_d[24 + j : 25 + j], sin_d[24 + j : 25 + j]
        cos_a[8 * j : 8 * j + 8] = (cj * cos_d[16:24] - sj * sin_d[16:24]).reshape(8, 1, bins)
        sin_a[8 * j : 8 * j + 8] = (sj * cos_d[16:24] + cj * sin_d[16:24]).reshape(8, 1, bins)

    turn = iota((1, PART), 1) & 3
    keep = jnp.where(turn == 0, 1.0, jnp.where(turn == 2, -1.0, 0.0))
    swap = jnp.where(turn == 1, 1.0, jnp.where(turn == 3, -1.0, 0.0))
    rec_halves[0:chans, :] = rec_ref[:, 0:half]
    rec_halves[chans : 2 * chans, :] = rec_ref[:, half:time_len]

    def fill(i, carry):
        at = pl.ds(pl.multiple_of(i * STEP, STEP), STEP)
        for q in range(chunks):
            part = slice(q * PART, (q + 1) * PART)
            ca, sa = cos_a[i, :, part], sin_a[i, :, part]
            cb, sb = cos_b[:, part], sin_b[:, part]
            tables[q][at, 0:PART] = (ca * cb - sa * sb).astype(BF16)
            tables[q][at, PART : 2 * PART] = (sa * cb + ca * sb).astype(BF16)
        return carry

    lax.fori_loop(0, steps, fill, 0)

    pl.semaphore_wait(barrier, nz - 1 + np_ - 1 + m - 1)

    spread_z(lambda z: zmeta_send.at[z], zmeta_recv, small_s.at[ZMETA], small_r.at[ZMETA])
    send_z(0)
    pack(1)
    send_z(1)

    power = jnp.zeros((chans, 1), F32)
    for q in range(chunks):
        sums = dot(rec_halves[...], tables[q][...])
        late_re, late_im = sums[chans:, :PART], sums[chans:, PART:]
        values = sums[:chans] + jnp.concatenate(
            [keep * late_re + swap * late_im, keep * late_im - swap * late_re], axis=1
        )
        spec[:, 2 * q * PART : 2 * (q + 1) * PART] = values
        power = power + jnp.sum(values * values, axis=1, keepdims=True)
    norm = jnp.sqrt(power / bins + 1e-6)

    wanted = jnp.sum(
        jnp.where(iota((sources, sources), 0) == iota((sources, sources), 1), vs_ref[...], 0),
        axis=1,
        keepdims=True,
    )
    chosen = one_hot(iota((sources, chans), 1) == wanted - me * chans)
    for q in range(chunks):
        pair = halves(spec[:, 2 * q * PART : (2 * q + 2) * PART] / norm)
        white[q, 0:chans, :], white[q, chans : 2 * chans, :] = pair
        src_send[q] = dot2(chosen, pair)

    spread_x(lambda p: src_send.at[p], src_mid, small_s.at[SRC1], small_r.at[SRC1])
    for q in range(2, chunks):
        pack(q)

    def forward_x(q):
        arrived(z_recv.at[q], zr_sem.at[q])
        block = jnp.concatenate(
            [
                z_recv[q, :, 0:room, :].reshape(z_rows, PART),
                z_recv[q, :, room : 2 * room, :].reshape(z_rows, PART),
            ],
            axis=1,
        )
        values = dot2(perm_ref[...], halves(block))
        x_send[q, :, 0:plane_slots, :] = values[:, :PART].reshape(np_, plane_slots, PART)
        x_send[q, :, plane_slots : 2 * plane_slots, :] = values[:, PART:].reshape(
            np_, plane_slots, PART
        )
        spread_x(lambda p: x_send.at[q, p], x_recv.at[q], xs_sem.at[q], xr_sem.at[q])

    def name_slots():
        arrived(xmeta_recv, small_r.at[XMETA])
        unfold_x = one_hot(lax.div(iota((slots, np_), 0), plane_slots) == iota((slots, np_), 1))
        metas = xmeta_recv[...].reshape(np_, 128)
        flag_send[...] = jnp.broadcast_to(
            jnp.max(jnp.where(iota((np_, 128), 1) == 100, metas, 0.0), keepdims=True), (1, 128)
        )
        spread(owners, in_column, lambda y: flag_send, flag_recv, small_s.at[FLAG], small_r.at[FLAG])
        wide = dot(unfold_x, metas.astype(BF16))
        lane_x = lax.rem(iota((slots, 128), 0), plane_slots)
        receiver = lanes_of(wide, lane_x).astype(jnp.int32) - 1
        source = lanes_of(wide, lane_x + plane_slots).astype(jnp.int32)
        hits = ones_where(iota((slots, chans), 1) == receiver)
        g_ref[:, 0:chans] = hits.astype(BF16)
        g_ref[:, chans : 2 * chans] = hits.astype(BF16)
        gt_ref[...] = hits.T.astype(BF16)
        named = lax.rem(iota((slots, 2 * sources), 1), sources) == source
        h_ref[...] = one_hot(named & (receiver >= 0))

    arrived(src_mid, small_r.at[SRC1])
    part = jnp.sum(src_mid[...], axis=0)
    few = sources // nz
    for z in range(nz):
        src_part[z] = part[z * few : (z + 1) * few]
    spread_z(lambda z: src_part.at[z], src_line, small_s.at[SRC2], small_r.at[SRC2])
    send_z(2)

    arrived(zmeta_recv, small_r.at[ZMETA])
    unfold_z = one_hot(lax.div(iota((z_rows, nz), 0), room) == iota((z_rows, nz), 1))
    metas = zmeta_recv[...].reshape(nz, 128)
    line_over = jnp.max(jnp.where(iota((nz, 128), 1) == 100, metas, 0.0), keepdims=True)
    wide = dot(unfold_z, metas.astype(BF16))
    code = lanes_of(wide, rank_z).astype(jnp.int32) - 1
    came_from = lax.div(iota((z_rows, 1), 0), room)
    to_plane = jnp.where(code >= 0, code >> 2, -1)
    within = came_from * CAP + (code & 3)
    target = jnp.where(code >= 0, to_plane * plane_slots + within, -1)
    perm_ref[...] = ones_where(iota((z_rows, slots), 1) == target).T.astype(BF16)
    to_plane_hot = ones_where(iota((z_rows, 128), 1) == to_plane)
    coded = jnp.where(lane_z == within, lanes_of(wide, rank_z + 32) + 1.0, 0.0) + jnp.where(
        lane_z == within + plane_slots, lanes_of(wide, rank_z + 64), 0.0
    )
    xmeta = dot(to_plane_hot.T[:np_].astype(BF16), coded.astype(BF16)) + jnp.where(
        iota((np_, 128), 1) == 100, line_over, 0.0
    )
    xmeta_send[...] = xmeta.reshape(np_, 1, 128)
    spread_x(lambda p: xmeta_send.at[p], xmeta_recv, small_s.at[XMETA], small_r.at[XMETA])

    arrived(src_line, small_r.at[SRC2])
    src_own[...] = jnp.sum(src_line[...], axis=0)
    spread_z(lambda z: src_own, src_rows, small_s.at[SRC3], small_r.at[SRC3])
    send_z(3)
    forward_x(0)
    name_slots()
    arrived(src_rows, small_r.at[SRC3])
    src_all[...] = jnp.concatenate([src_rows[z] for z in range(nz)], axis=0)
    spread_x(lambda p: src_all, src_recv, small_s.at[SRC4], small_r.at[SRC4])
    for q in range(4, min(6, chunks)):
        send_z(q)
    forward_x(1)
    arrived(src_recv, small_r.at[SRC4])

    mis_acc[...] = jnp.zeros_like(mis_acc)

    def correlate(q):
        arrived(x_recv.at[q], xr_sem.at[q])
        band = (q * PART + iota((1, PART), 1)).astype(F32)
        taper = 0.5 - 0.5 * jnp.cos((band + 0.5) * (2.0 * math.pi / bins))
        source_rows = dot(h_ref[...], jnp.concatenate(halves(src_recv[q]), axis=0))
        receiver_rows = dot(g_ref[...], white[q])
        s_re, s_im = source_rows[:, :PART], source_rows[:, PART:]
        r_re, r_im = receiver_rows[:, :PART], receiver_rows[:, PART:]
        d_re = s_re * r_re + s_im * r_im - x_recv[q, :, 0:plane_slots, :].reshape(slots, PART)
        d_im = s_re * r_im - s_im * r_re - x_recv[q, :, plane_slots : 2 * plane_slots, :].reshape(
            slots, PART
        )
        e_re, e_im = taper * d_re, taper * d_im
        mis_acc[...] += e_re * d_re + e_im * d_im
        terms = jnp.concatenate([e_re * s_re - e_im * s_im, e_re * s_im + e_im * s_re], axis=1)
        adj_send[q] = dot2(gt_ref[...], halves(terms)).reshape(m, rows_out, 2 * PART)
        spread(
            owners,
            in_column,
            lambda y: adj_send.at[q, y],
            adj_recv.at[q],
            ys_sem.at[q],
            yr_sem.at[q],
        )

    def inverse(q):
        arrived(adj_recv.at[q], yr_sem.at[q])
        total = adj_recv[q, 0]
        for y in range(1, m):
            total = total + adj_recv[q, y]
        total = total * (1.0 / math.sqrt(bins))
        real, imaginary = total[:, :PART], total[:, PART:]
        late = jnp.concatenate(
            [keep * real - swap * imaginary, swap * real + keep * imaginary], axis=1
        )
        both = jnp.concatenate(halves(jnp.concatenate([total, late], axis=0)), axis=0)
        span = min(512, half)

        def one(i, carry):
            at = pl.ds(pl.multiple_of(i * span, span), span)
            after = pl.ds(pl.multiple_of(half + i * span, span), span)
            product = dot_t(both, tables[q][at, :])
            values = product[: 2 * rows_out] + product[2 * rows_out :]
            if q == 0:
                out_ref[:, at] = values[:rows_out]
                out_ref[:, after] = values[rows_out:]
            else:
                out_ref[:, at] += values[:rows_out]
                out_ref[:, after] += values[rows_out:]
            return carry

        lax.fori_loop(0, half // span, one, 0)

    for q in range(chunks):
        correlate(q)
        if q + 6 < chunks:
            send_z(q + 6)
        if q + 2 < chunks:
            forward_x(q + 2)
        if 2 <= q < chunks - 1:
            inverse(q - 2)

    lane_4 = iota((slots, 128), 0) & 3
    total = jnp.sum(mis_acc[...], axis=1, keepdims=True) * (0.5 / bins)
    count = nz * np_
    fold_4 = one_hot(iota((count, slots), 0) == (iota((count, slots), 1) >> 2))
    spread_out = jnp.where(iota((slots, 128), 1) == lane_4, total, 0.0)
    mis_send[...] = dot2(fold_4, halves(spread_out)).reshape(count, 1, 128)

    spread(
        [plane_ids[i] * nz + line[j] for i in range(np_) for j in range(nz)],
        [there(i, j) for i in range(np_) for j in range(nz)],
        lambda u: mis_send.at[u],
        mis_recv,
        small_s.at[MIS],
        small_r.at[MIS],
    )
    for q in range(max(0, chunks - 3), chunks):
        inverse(q)

    arrived(mis_recv, small_r.at[MIS])
    unfold_4 = one_hot((iota((slots, count), 0) >> 2) == iota((slots, count), 1))
    back = dot2(unfold_4, halves(mis_recv[...].reshape(count, 128)))
    own = ones_where((plane * nz + slab) * CAP + rank == iota((slots, pairs), 0))
    mis_ref[...] = jnp.sum(own * lanes_of(back, lane_4), axis=0, keepdims=True)
    arrived(flag_recv, small_r.at[FLAG])
    over_ref[...] = jnp.max(flag_recv[...], axis=0)

    for q in range(chunks):
        left(z_recv.at[q], zs_sem.at[q])
        left(x_recv.at[q], xs_sem.at[q])
        left(adj_recv.at[q], ys_sem.at[q])
    for recv, sem in (
        (zmeta_recv, ZMETA),
        (xmeta_recv, XMETA),
        (src_mid, SRC1),
        (src_line, SRC2),
        (src_rows, SRC3),
        (src_recv, SRC4),
        (mis_recv, MIS),
        (flag_recv, FLAG),
    ):
        left(recv, small_s.at[sem])


def exchange(nz, np_, m, room, number, operands):
    records, observed = operands[0], operands[5]
    chans, time_len = records.shape
    pairs, width = observed.shape
    bins = width // 2
    chunks = bins // PART
    rows_out = chans // m
    sources = operands[1].shape[1]
    slots = np_ * nz * CAP
    assert chunks == np_
    vmem = pltpu.VMEM
    return pl.pallas_call(
        functools.partial(kernel, nz, np_, m, room),
        out_shape=(
            jax.ShapeDtypeStruct((rows_out, time_len), F32),
            jax.ShapeDtypeStruct((1, pairs), F32),
            jax.ShapeDtypeStruct((1, 128), F32),
        ),
        in_specs=[pl.BlockSpec(memory_space=vmem)] * 6,
        out_specs=(pl.BlockSpec(memory_space=vmem),) * 3,
        scratch_shapes=[
            vmem((chunks, nz, 2 * room, PART), F32),
            vmem((chunks, nz, 2 * room, PART), F32),
            vmem((chunks, np_, 2 * nz * CAP, PART), F32),
            vmem((chunks, np_, 2 * nz * CAP, PART), F32),
            vmem((nz, 1, 128), F32),
            vmem((nz, 1, 128), F32),
            vmem((np_, 1, 128), F32),
            vmem((np_, 1, 128), F32),
            vmem((np_, sources, 2 * PART), F32),
            vmem((np_, sources, 2 * PART), F32),
            vmem((nz, sources // nz, 2 * PART), F32),
            vmem((nz, sources // nz, 2 * PART), F32),
            vmem((sources // nz, 2 * PART), F32),
            vmem((nz, sources // nz, 2 * PART), F32),
            vmem((sources, 2 * PART), F32),
            vmem((np_, sources, 2 * PART), F32),
            vmem((chunks, m, rows_out, 2 * PART), F32),
            vmem((chunks, m, rows_out, 2 * PART), F32),
            vmem((nz * np_, 1, 128), F32),
            vmem((nz * np_, 1, 128), F32),
            vmem((1, 128), F32),
            vmem((m, 1, 128), F32),
            vmem((2 * chans, time_len // 2), BF16),
            [vmem((time_len // 2, 2 * PART), BF16) for _ in range(chunks)],
            vmem((time_len // 2 // STEP, 1, bins), F32),
            vmem((time_len // 2 // STEP, 1, bins), F32),
            vmem((STEP, bins), F32),
            vmem((STEP, bins), F32),
            vmem((chans, width), F32),
            vmem((chunks, 2 * chans, 2 * PART), BF16),
            vmem((slots, nz * room), BF16),
            vmem((slots, 2 * chans), BF16),
            vmem((chans, slots), BF16),
            vmem((slots, 2 * sources), BF16),
            vmem((slots, PART), F32),
            pltpu.SemaphoreType.DMA((chunks,)),
            pltpu.SemaphoreType.DMA((chunks,)),
            pltpu.SemaphoreType.DMA((chunks,)),
            pltpu.SemaphoreType.DMA((chunks,)),
            pltpu.SemaphoreType.DMA((chunks,)),
            pltpu.SemaphoreType.DMA((chunks,)),
            pltpu.SemaphoreType.DMA((8,)),
            pltpu.SemaphoreType.DMA((8,)),
        ],
        compiler_params=pltpu.CompilerParams(
            collective_id=number, has_side_effects=True, vmem_limit_bytes=56 * 1024 * 1024
        ),
    )(*operands)


def per_device(n, m, records, virtual_sources, pair_group, pair_receiver, pair_source, observed):
    pairs, width = observed.shape
    np_ = width // 2 // PART
    nz = n // np_
    most = np_ * CAP
    usual = max(8, most * 3 // 4 // 8 * 8)
    operands = (
        records,
        virtual_sources.reshape(1, -1),
        pair_group.reshape(1, pairs),
        pair_receiver.reshape(1, pairs),
        pair_source.reshape(1, pairs),
        observed,
    )
    adjoint, misfit, over = exchange(nz, np_, m, usual, 0, operands)
    adjoint, misfit = lax.cond(
        over[0, 0] > 0.0,
        lambda held: exchange(nz, np_, m, most, 1, operands)[:2],
        lambda held: held,
        (adjoint, misfit),
    )
    return adjoint, misfit.reshape(pairs)


def solution(mesh):
    return jax.shard_map(
        functools.partial(per_device, mesh.shape["chan"], mesh.shape["src"]),
        mesh=mesh,
        in_specs=(
            P("chan", None),
            P("src"),
            P(("chan", "src"), None),
            P(("chan", "src")),
            P(("chan", "src")),
            P(("chan", "src"), None),
        ),
        out_specs=(P(("chan", "src"), None), P(("chan", "src"))),
        check_vma=False,
    )
```

```python
import functools
import math

import jax
import jax.numpy as jnp
from jax import lax
from jax.experimental import pallas as pl
from jax.experimental.pallas import tpu as pltpu
from jax.sharding import PartitionSpec as P

K0 = 64
CAP = 4
STEP = 64
PART = 128
MESH = pl.DeviceIdType.MESH
F32 = jnp.float32
BF16 = jnp.bfloat16


def iota(shape, axis):
    return lax.broadcasted_iota(jnp.int32, shape, axis)


def ones_where(mask):
    return jnp.where(mask, 1.0, 0.0)


def one_hot(mask):
    return ones_where(mask).astype(BF16)


def dot(left, right):
    return jnp.dot(left, right, preferred_element_type=F32)


def dot_t(left, right):
    return lax.dot_general(left, right, (((1,), (1,)), ((), ())), preferred_element_type=F32)


def halves(value):
    high = value.astype(BF16)
    return high, (value - high.astype(F32)).astype(BF16)


def dot2(left, pair):
    return dot(left, pair[0]) + dot(left, pair[1])


def both_ways(size):
    steps = [0]
    for i in range(1, size // 2 + 1):
        steps += [i] if 2 * i == size else [i, size - i]
    return steps


def lanes_of(values, lane):
    return jnp.sum(jnp.where(iota(values.shape, 1) == lane, values, 0.0), axis=1, keepdims=True)


def kernel(
    nz,
    np_,
    m,
    room,
    rec_ref,
    vs_ref,
    group_ref,
    prec_ref,
    psrc_ref,
    obs_ref,
    out_ref,
    mis_ref,
    over_ref,
    z_send,
    z_recv,
    x_send,
    x_recv,
    zmeta_send,
    zmeta_recv,
    xmeta_send,
    xmeta_recv,
    src_send,
    src_mid,
    src_part,
    src_line,
    src_own,
    src_rows,
    src_all,
    src_recv,
    adj_send,
    adj_recv,
    mis_send,
    mis_recv,
    flag_send,
    flag_recv,
    rec_halves,
    tables,
    cos_a,
    sin_a,
    cos_b,
    sin_b,
    spec,
    white,
    perm_ref,
    g_ref,
    gt_ref,
    h_ref,
    mis_acc,
    zs_sem,
    zr_sem,
    xs_sem,
    xr_sem,
    ys_sem,
    yr_sem,
    small_s,
    small_r,
):
    chans, time_len = rec_ref.shape
    pairs, width = obs_ref.shape
    bins = width // 2
    chunks = bins // PART
    rows_out = chans // m
    sources = vs_ref.shape[1]
    z_rows = nz * room
    plane_slots = nz * CAP
    slots = np_ * plane_slots
    me = lax.axis_index("chan")
    owner = lax.axis_index("src")
    my_z = lax.rem(lax.div(me, 2), nz)
    my_p = lax.div(me, 2 * nz) * 2 + lax.rem(me, 2)
    nx = np_ // 2
    my_x, my_core = lax.div(me, 2 * nz), lax.rem(me, 2)
    line = [lax.rem(my_z + i, nz) for i in both_ways(nz)]
    plane_ids = [
        lax.rem(my_x + i, nx) * 2 + lax.rem(my_core + c, 2)
        for i in both_ways(nx)
        for c in range(2)
    ]
    owners = [lax.rem(owner + i, m) for i in range(m)]
    base = [lax.div(p, 2) * (2 * nz) + lax.rem(p, 2) for p in plane_ids]

    def there(i, j):
        return {"chan": base[i] + 2 * line[j]}

    on_line = [there(0, j) for j in range(nz)]
    in_plane = [there(i, 0) for i in range(np_)]
    in_column = [{"src": y} for y in owners]

    barrier = pltpu.get_barrier_semaphore()
    for devices in (on_line, in_plane, in_column):
        for device in devices[1:]:
            pl.semaphore_signal(barrier, inc=1, device_id=device, device_id_type=MESH)

    def spread(places, devices, send, recv, send_sem, recv_sem):
        mine = places[0]
        for place, device in zip(places[1:], devices[1:]):
            pltpu.make_async_remote_copy(
                src_ref=send(place),
                dst_ref=recv.at[mine],
                send_sem=send_sem,
                recv_sem=recv_sem,
                device_id=device,
                device_id_type=MESH,
            ).start()
        pltpu.make_async_copy(send(mine), recv.at[mine], recv_sem).start()

    def arrived(recv, sem):
        pltpu.make_async_copy(recv, recv, sem).wait()

    def left(recv, sem):
        some = recv.at[pl.ds(0, recv.shape[0] - 1)]
        pltpu.make_async_copy(some, some, sem).wait()

    def spread_z(send, recv, send_sem, recv_sem):
        spread(line, on_line, send, recv, send_sem, recv_sem)

    def spread_x(send, recv, send_sem, recv_sem):
        spread(plane_ids, in_plane, send, recv, send_sem, recv_sem)

    ZMETA, XMETA, SRC1, SRC2, SRC3, SRC4, MIS, FLAG = range(8)

    diagonal = iota((pairs, pairs), 0) == iota((pairs, pairs), 1)
    earlier = iota((pairs, pairs), 0) < iota((pairs, pairs), 1)
    group = group_ref[...]
    group_col = jnp.sum(jnp.where(diagonal, group, 0), axis=1, keepdims=True)
    rank = jnp.sum(jnp.where((group_col == group) & earlier, 1, 0), axis=0, keepdims=True)
    slab = lax.rem(group >> 1, nz)
    slab_col = lax.rem(group_col >> 1, nz)
    place = jnp.sum(jnp.where((slab_col == slab) & earlier, 1, 0), axis=0, keepdims=True)
    plane = lax.div(group, 2 * nz) * 2 + (group & 1)
    over = jnp.max(jnp.where(place >= room, 1.0, 0.0), axis=1, keepdims=True)
    row = jnp.where(place < room, slab * room + place, -1)
    pick = ones_where(row == iota((z_rows, pairs), 0))
    pick_bf = jnp.concatenate([pick, pick], axis=1).astype(BF16)

    def pack(q):
        block = jnp.concatenate(
            [
                obs_ref[:, q * PART : (q + 1) * PART],
                obs_ref[:, bins + q * PART : bins + (q + 1) * PART],
            ],
            axis=1,
        )
        values = dot(pick_bf, jnp.concatenate(halves(block), axis=0))
        z_send[q, :, 0:room, :] = values[:, :PART].reshape(nz, room, PART)
        z_send[q, :, room : 2 * room, :] = values[:, PART:].reshape(nz, room, PART)

    def send_z(q):
        spread_z(lambda z: z_send.at[q, z], z_recv.at[q], zs_sem.at[q], zr_sem.at[q])

    pack(0)
    lane_z = iota((z_rows, 128), 1)
    rank_z = lax.rem(iota((z_rows, 128), 0), room)

    def along(values):
        return jnp.sum(jnp.where(pick > 0.5, values.astype(F32), 0.0), axis=1, keepdims=True)

    coded = (
        jnp.where(lane_z == rank_z, along(plane * CAP + rank + 1), 0.0)
        + jnp.where(lane_z == rank_z + 32, along(prec_ref[...]), 0.0)
        + jnp.where(lane_z == rank_z + 64, along(psrc_ref[...]), 0.0)
    )
    fold_z = one_hot(
        iota((nz, z_rows), 0) == lax.div(iota((nz, z_rows), 1), room)
    )
    zmeta = dot(fold_z, coded.astype(BF16)) + jnp.where(iota((nz, 128), 1) == 100, over, 0.0)
    zmeta_send[...] = zmeta.reshape(nz, 1, 128)

    half = time_len // 2
    steps = half // STEP
    digit = iota((32, bins), 0) >> 3
    times = (iota((32, bins), 0) & 7) * jnp.where(
        digit == 0, 1, jnp.where(digit == 1, 8, jnp.where(digit == 2, 64, 512))
    )
    phase = ((K0 + iota((32, bins), 1)) * times) & (2 * time_len - 1)
    angle = phase.astype(F32) * (math.pi / time_len)
    cos_d, sin_d = jnp.cos(angle), -jnp.sin(angle)
    for j in range(8):
        cj, sj = cos_d[8 + j : 9 + j], sin_d[8 + j : 9 + j]
        cos_b[8 * j : 8 * j + 8, :] = cj * cos_d[:8] - sj * sin_d[:8]
        sin_b[8 * j : 8 * j + 8, :] = sj * cos_d[:8] + cj * sin_d[:8]
    for j in range(steps // 8):
        cj, sj = cos_d[24 + j : 25 + j], sin_d[24 + j : 25 + j]
        cos_a[8 * j : 8 * j + 8] = (cj * cos_d[16:24] - sj * sin_d[16:24]).reshape(8, 1, bins)
        sin_a[8 * j : 8 * j + 8] = (sj * cos_d[16:24] + cj * sin_d[16:24]).reshape(8, 1, bins)

    turn = iota((1, PART), 1) & 3
    keep = jnp.where(turn == 0, 1.0, jnp.where(turn == 2, -1.0, 0.0))
    swap = jnp.where(turn == 1, 1.0, jnp.where(turn == 3, -1.0, 0.0))
    rec_halves[0:chans, :] = rec_ref[:, 0:half]
    rec_halves[chans : 2 * chans, :] = rec_ref[:, half:time_len]

    def fill(i, carry):
        at = pl.ds(pl.multiple_of(i * STEP, STEP), STEP)
        for q in range(chunks):
            part = slice(q * PART, (q + 1) * PART)
            ca, sa = cos_a[i, :, part], sin_a[i, :, part]
            cb, sb = cos_b[:, part], sin_b[:, part]
            tables[q][at, 0:PART] = (ca * cb - sa * sb).astype(BF16)
            tables[q][at, PART : 2 * PART] = (sa * cb + ca * sb).astype(BF16)
        return carry

    lax.fori_loop(0, steps, fill, 0)

    pl.semaphore_wait(barrier, nz - 1 + np_ - 1 + m - 1)

    spread_z(lambda z: zmeta_send.at[z], zmeta_recv, small_s.at[ZMETA], small_r.at[ZMETA])
    send_z(0)
    pack(1)
    send_z(1)

    power = jnp.zeros((chans, 1), F32)
    for q in range(chunks):
        sums = dot(rec_halves[...], tables[q][...])
        late_re, late_im = sums[chans:, :PART], sums[chans:, PART:]
        values = sums[:chans] + jnp.concatenate(
            [keep * late_re + swap * late_im, keep * late_im - swap * late_re], axis=1
        )
        spec[:, 2 * q * PART : 2 * (q + 1) * PART] = values
        power = power + jnp.sum(values * values, axis=1, keepdims=True)
    norm = jnp.sqrt(power / bins + 1e-6)

    wanted = jnp.sum(
        jnp.where(iota((sources, sources), 0) == iota((sources, sources), 1), vs_ref[...], 0),
        axis=1,
        keepdims=True,
    )
    chosen = one_hot(iota((sources, chans), 1) == wanted - me * chans)
    for q in range(chunks):
        pair = halves(spec[:, 2 * q * PART : (2 * q + 2) * PART] / norm)
        white[q, 0:chans, :], white[q, chans : 2 * chans, :] = pair
        src_send[q] = dot2(chosen, pair)

    spread_x(lambda p: src_send.at[p], src_mid, small_s.at[SRC1], small_r.at[SRC1])
    for q in range(2, chunks):
        pack(q)

    def forward_x(q):
        arrived(z_recv.at[q], zr_sem.at[q])
        block = jnp.concatenate(
            [
                z_recv[q, :, 0:room, :].reshape(z_rows, PART),
                z_recv[q, :, room : 2 * room, :].reshape(z_rows, PART),
            ],
            axis=1,
        )
        values = dot2(perm_ref[...], halves(block))
        x_send[q, :, 0:plane_slots, :] = values[:, :PART].reshape(np_, plane_slots, PART)
        x_send[q, :, plane_slots : 2 * plane_slots, :] = values[:, PART:].reshape(
            np_, plane_slots, PART
        )
        spread_x(lambda p: x_send.at[q, p], x_recv.at[q], xs_sem.at[q], xr_sem.at[q])

    def name_slots():
        arrived(xmeta_recv, small_r.at[XMETA])
        unfold_x = one_hot(lax.div(iota((slots, np_), 0), plane_slots) == iota((slots, np_), 1))
        metas = xmeta_recv[...].reshape(np_, 128)
        flag_send[...] = jnp.broadcast_to(
            jnp.max(jnp.where(iota((np_, 128), 1) == 100, metas, 0.0), keepdims=True), (1, 128)
        )
        spread(owners, in_column, lambda y: flag_send, flag_recv, small_s.at[FLAG], small_r.at[FLAG])
        wide = dot(unfold_x, metas.astype(BF16))
        lane_x = lax.rem(iota((slots, 128), 0), plane_slots)
        receiver = lanes_of(wide, lane_x).astype(jnp.int32) - 1
        source = lanes_of(wide, lane_x + plane_slots).astype(jnp.int32)
        hits = ones_where(iota((slots, chans), 1) == receiver)
        g_ref[:, 0:chans] = hits.astype(BF16)
        g_ref[:, chans : 2 * chans] = hits.astype(BF16)
        gt_ref[...] = hits.T.astype(BF16)
        named = lax.rem(iota((slots, 2 * sources), 1), sources) == source
        h_ref[...] = one_hot(named & (receiver >= 0))

    arrived(src_mid, small_r.at[SRC1])
    part = jnp.sum(src_mid[...], axis=0)
    few = sources // nz
    for z in range(nz):
        src_part[z] = part[z * few : (z + 1) * few]
    spread_z(lambda z: src_part.at[z], src_line, small_s.at[SRC2], small_r.at[SRC2])
    send_z(2)

    arrived(zmeta_recv, small_r.at[ZMETA])
    unfold_z = one_hot(lax.div(iota((z_rows, nz), 0), room) == iota((z_rows, nz), 1))
    metas = zmeta_recv[...].reshape(nz, 128)
    line_over = jnp.max(jnp.where(iota((nz, 128), 1) == 100, metas, 0.0), keepdims=True)
    wide = dot(unfold_z, metas.astype(BF16))
    code = lanes_of(wide, rank_z).astype(jnp.int32) - 1
    came_from = lax.div(iota((z_rows, 1), 0), room)
    to_plane = jnp.where(code >= 0, code >> 2, -1)
    within = came_from * CAP + (code & 3)
    target = jnp.where(code >= 0, to_plane * plane_slots + within, -1)
    perm_ref[...] = ones_where(iota((z_rows, slots), 1) == target).T.astype(BF16)
    to_plane_hot = ones_where(iota((z_rows, 128), 1) == to_plane)
    coded = jnp.where(lane_z == within, lanes_of(wide, rank_z + 32) + 1.0, 0.0) + jnp.where(
        lane_z == within + plane_slots, lanes_of(wide, rank_z + 64), 0.0
    )
    xmeta = dot(to_plane_hot.T[:np_].astype(BF16), coded.astype(BF16)) + jnp.where(
        iota((np_, 128), 1) == 100, line_over, 0.0
    )
    xmeta_send[...] = xmeta.reshape(np_, 1, 128)
    spread_x(lambda p: xmeta_send.at[p], xmeta_recv, small_s.at[XMETA], small_r.at[XMETA])

    arrived(src_line, small_r.at[SRC2])
    src_own[...] = jnp.sum(src_line[...], axis=0)
    spread_z(lambda z: src_own, src_rows, small_s.at[SRC3], small_r.at[SRC3])
    send_z(3)
    forward_x(0)
    forward_x(1)
    name_slots()
    arrived(src_rows, small_r.at[SRC3])
    src_all[...] = jnp.concatenate([src_rows[z] for z in range(nz)], axis=0)
    spread_x(lambda p: src_all, src_recv, small_s.at[SRC4], small_r.at[SRC4])
    for q in range(4, min(6, chunks)):
        send_z(q)
    forward_x(2)
    arrived(src_recv, small_r.at[SRC4])

    mis_acc[...] = jnp.zeros_like(mis_acc)

    def correlate(q):
        arrived(x_recv.at[q], xr_sem.at[q])
        band = (q * PART + iota((1, PART), 1)).astype(F32)
        taper = 0.5 - 0.5 * jnp.cos((band + 0.5) * (2.0 * math.pi / bins))
        source_rows = dot(h_ref[...], jnp.concatenate(halves(src_recv[q]), axis=0))
        receiver_rows = dot(g_ref[...], white[q])
        s_re, s_im = source_rows[:, :PART], source_rows[:, PART:]
        r_re, r_im = receiver_rows[:, :PART], receiver_rows[:, PART:]
        d_re = s_re * r_re + s_im * r_im - x_recv[q, :, 0:plane_slots, :].reshape(slots, PART)
        d_im = s_re * r_im - s_im * r_re - x_recv[q, :, plane_slots : 2 * plane_slots, :].reshape(
            slots, PART
        )
        e_re, e_im = taper * d_re, taper * d_im
        mis_acc[...] += e_re * d_re + e_im * d_im
        terms = jnp.concatenate([e_re * s_re - e_im * s_im, e_re * s_im + e_im * s_re], axis=1)
        adj_send[q] = dot2(gt_ref[...], halves(terms)).reshape(m, rows_out, 2 * PART)
        spread(
            owners,
            in_column,
            lambda y: adj_send.at[q, y],
            adj_recv.at[q],
            ys_sem.at[q],
            yr_sem.at[q],
        )

    def inverse(q):
        arrived(adj_recv.at[q], yr_sem.at[q])
        total = adj_recv[q, 0]
        for y in range(1, m):
            total = total + adj_recv[q, y]
        total = total * (1.0 / math.sqrt(bins))
        real, imaginary = total[:, :PART], total[:, PART:]
        late = jnp.concatenate(
            [keep * real - swap * imaginary, swap * real + keep * imaginary], axis=1
        )
        both = jnp.concatenate(halves(jnp.concatenate([total, late], axis=0)), axis=0)
        span = min(512, half)

        def one(i, carry):
            at = pl.ds(pl.multiple_of(i * span, span), span)
            after = pl.ds(pl.multiple_of(half + i * span, span), span)
            product = dot_t(both, tables[q][at, :])
            values = product[: 2 * rows_out] + product[2 * rows_out :]
            if q == 0:
                out_ref[:, at] = values[:rows_out]
                out_ref[:, after] = values[rows_out:]
            else:
                out_ref[:, at] += values[:rows_out]
                out_ref[:, after] += values[rows_out:]
            return carry

        lax.fori_loop(0, half // span, one, 0)

    for q in range(chunks):
        correlate(q)
        if q + 6 < chunks:
            send_z(q + 6)
        if q + 3 < chunks:
            forward_x(q + 3)
        if 2 <= q < chunks - 1:
            inverse(q - 2)

    lane_4 = iota((slots, 128), 0) & 3
    total = jnp.sum(mis_acc[...], axis=1, keepdims=True) * (0.5 / bins)
    count = nz * np_
    fold_4 = one_hot(iota((count, slots), 0) == (iota((count, slots), 1) >> 2))
    spread_out = jnp.where(iota((slots, 128), 1) == lane_4, total, 0.0)
    mis_send[...] = dot2(fold_4, halves(spread_out)).reshape(count, 1, 128)

    spread(
        [plane_ids[i] * nz + line[j] for i in range(np_) for j in range(nz)],
        [there(i, j) for i in range(np_) for j in range(nz)],
        lambda u: mis_send.at[u],
        mis_recv,
        small_s.at[MIS],
        small_r.at[MIS],
    )
    for q in range(max(0, chunks - 3), chunks):
        inverse(q)

    arrived(mis_recv, small_r.at[MIS])
    unfold_4 = one_hot((iota((slots, count), 0) >> 2) == iota((slots, count), 1))
    back = dot2(unfold_4, halves(mis_recv[...].reshape(count, 128)))
    own = ones_where((plane * nz + slab) * CAP + rank == iota((slots, pairs), 0))
    mis_ref[...] = jnp.sum(own * lanes_of(back, lane_4), axis=0, keepdims=True)
    arrived(flag_recv, small_r.at[FLAG])
    over_ref[...] = jnp.max(flag_recv[...], axis=0)

    for q in range(chunks):
        left(z_recv.at[q], zs_sem.at[q])
        left(x_recv.at[q], xs_sem.at[q])
        left(adj_recv.at[q], ys_sem.at[q])
    for recv, sem in (
        (zmeta_recv, ZMETA),
        (xmeta_recv, XMETA),
        (src_mid, SRC1),
        (src_line, SRC2),
        (src_rows, SRC3),
        (src_recv, SRC4),
        (mis_recv, MIS),
        (flag_recv, FLAG),
    ):
        left(recv, small_s.at[sem])


def exchange(nz, np_, m, room, number, operands):
    records, observed = operands[0], operands[5]
    chans, time_len = records.shape
    pairs, width = observed.shape
    bins = width // 2
    chunks = bins // PART
    rows_out = chans // m
    sources = operands[1].shape[1]
    slots = np_ * nz * CAP
    assert chunks == np_
    vmem = pltpu.VMEM
    return pl.pallas_call(
        functools.partial(kernel, nz, np_, m, room),
        out_shape=(
            jax.ShapeDtypeStruct((rows_out, time_len), F32),
            jax.ShapeDtypeStruct((1, pairs), F32),
            jax.ShapeDtypeStruct((1, 128), F32),
        ),
        in_specs=[pl.BlockSpec(memory_space=vmem)] * 6,
        out_specs=(pl.BlockSpec(memory_space=vmem),) * 3,
        scratch_shapes=[
            vmem((chunks, nz, 2 * room, PART), F32),
            vmem((chunks, nz, 2 * room, PART), F32),
            vmem((chunks, np_, 2 * nz * CAP, PART), F32),
            vmem((chunks, np_, 2 * nz * CAP, PART), F32),
            vmem((nz, 1, 128), F32),
            vmem((nz, 1, 128), F32),
            vmem((np_, 1, 128), F32),
            vmem((np_, 1, 128), F32),
            vmem((np_, sources, 2 * PART), F32),
            vmem((np_, sources, 2 * PART), F32),
            vmem((nz, sources // nz, 2 * PART), F32),
            vmem((nz, sources // nz, 2 * PART), F32),
            vmem((sources // nz, 2 * PART), F32),
            vmem((nz, sources // nz, 2 * PART), F32),
            vmem((sources, 2 * PART), F32),
            vmem((np_, sources, 2 * PART), F32),
            vmem((chunks, m, rows_out, 2 * PART), F32),
            vmem((chunks, m, rows_out, 2 * PART), F32),
            vmem((nz * np_, 1, 128), F32),
            vmem((nz * np_, 1, 128), F32),
            vmem((1, 128), F32),
            vmem((m, 1, 128), F32),
            vmem((2 * chans, time_len // 2), BF16),
            [vmem((time_len // 2, 2 * PART), BF16) for _ in range(chunks)],
            vmem((time_len // 2 // STEP, 1, bins), F32),
            vmem((time_len // 2 // STEP, 1, bins), F32),
            vmem((STEP, bins), F32),
            vmem((STEP, bins), F32),
            vmem((chans, width), F32),
            vmem((chunks, 2 * chans, 2 * PART), BF16),
            vmem((slots, nz * room), BF16),
            vmem((slots, 2 * chans), BF16),
            vmem((chans, slots), BF16),
            vmem((slots, 2 * sources), BF16),
            vmem((slots, PART), F32),
            pltpu.SemaphoreType.DMA((chunks,)),
            pltpu.SemaphoreType.DMA((chunks,)),
            pltpu.SemaphoreType.DMA((chunks,)),
            pltpu.SemaphoreType.DMA((chunks,)),
            pltpu.SemaphoreType.DMA((chunks,)),
            pltpu.SemaphoreType.DMA((chunks,)),
            pltpu.SemaphoreType.DMA((8,)),
            pltpu.SemaphoreType.DMA((8,)),
        ],
        compiler_params=pltpu.CompilerParams(
            collective_id=number, has_side_effects=True, vmem_limit_bytes=56 * 1024 * 1024
        ),
    )(*operands)


def per_device(n, m, records, virtual_sources, pair_group, pair_receiver, pair_source, observed):
    pairs, width = observed.shape
    np_ = width // 2 // PART
    nz = n // np_
    most = np_ * CAP
    usual = max(8, most * 3 // 4 // 8 * 8)
    operands = (
        records,
        virtual_sources.reshape(1, -1),
        pair_group.reshape(1, pairs),
        pair_receiver.reshape(1, pairs),
        pair_source.reshape(1, pairs),
        observed,
    )
    adjoint, misfit, over = exchange(nz, np_, m, usual, 0, operands)
    adjoint, misfit = lax.cond(
        over[0, 0] > 0.0,
        lambda held: exchange(nz, np_, m, most, 1, operands)[:2],
        lambda held: held,
        (adjoint, misfit),
    )
    return adjoint, misfit.reshape(pairs)


def solution(mesh):
    return jax.shard_map(
        functools.partial(per_device, mesh.shape["chan"], mesh.shape["src"]),
        mesh=mesh,
        in_specs=(
            P("chan", None),
            P("src"),
            P(("chan", "src"), None),
            P(("chan", "src")),
            P(("chan", "src")),
            P(("chan", "src"), None),
        ),
        out_specs=(P(("chan", "src"), None), P(("chan", "src"))),
        check_vma=False,
    )
```

```python
import functools
import math

import jax
import jax.numpy as jnp
from jax import lax
from jax.experimental import pallas as pl
from jax.experimental.pallas import tpu as pltpu
from jax.sharding import PartitionSpec as P

K0 = 64
CAP = 4
STEP = 64
PART = 128
MESH = pl.DeviceIdType.MESH
F32 = jnp.float32
BF16 = jnp.bfloat16


def iota(shape, axis):
    return lax.broadcasted_iota(jnp.int32, shape, axis)


def ones_where(mask):
    return jnp.where(mask, 1.0, 0.0)


def one_hot(mask):
    return ones_where(mask).astype(BF16)


def dot(left, right):
    return jnp.dot(left, right, preferred_element_type=F32)


def dot_t(left, right):
    return lax.dot_general(left, right, (((1,), (1,)), ((), ())), preferred_element_type=F32)


def halves(value):
    high = value.astype(BF16)
    return high, (value - high.astype(F32)).astype(BF16)


def dot2(left, pair):
    return dot(left, pair[0]) + dot(left, pair[1])


def both_ways(size):
    steps = [0]
    for i in range(1, size // 2 + 1):
        steps += [i] if 2 * i == size else [i, size - i]
    return steps


def lanes_of(values, lane):
    return jnp.sum(jnp.where(iota(values.shape, 1) == lane, values, 0.0), axis=1, keepdims=True)


def kernel(
    nz,
    np_,
    m,
    room,
    rec_ref,
    vs_ref,
    group_ref,
    prec_ref,
    psrc_ref,
    obs_ref,
    out_ref,
    mis_ref,
    over_ref,
    z_send,
    z_recv,
    x_send,
    x_recv,
    zmeta_send,
    zmeta_recv,
    xmeta_send,
    xmeta_recv,
    src_send,
    src_mid,
    src_part,
    src_line,
    src_own,
    src_rows,
    src_all,
    src_recv,
    adj_send,
    adj_recv,
    mis_send,
    mis_recv,
    flag_send,
    flag_recv,
    rec_halves,
    tables,
    cos_a,
    sin_a,
    cos_b,
    sin_b,
    spec,
    white,
    perm_ref,
    g_ref,
    gt_ref,
    h_ref,
    mis_acc,
    zs_sem,
    zr_sem,
    xs_sem,
    xr_sem,
    ys_sem,
    yr_sem,
    small_s,
    small_r,
):
    chans, time_len = rec_ref.shape
    pairs, width = obs_ref.shape
    bins = width // 2
    chunks = bins // PART
    rows_out = chans // m
    sources = vs_ref.shape[1]
    z_rows = nz * room
    plane_slots = nz * CAP
    slots = np_ * plane_slots
    me = lax.axis_index("chan")
    owner = lax.axis_index("src")
    my_z = lax.rem(lax.div(me, 2), nz)
    my_p = lax.div(me, 2 * nz) * 2 + lax.rem(me, 2)
    nx = np_ // 2
    my_x, my_core = lax.div(me, 2 * nz), lax.rem(me, 2)
    line = [lax.rem(my_z + i, nz) for i in both_ways(nz)]
    plane_ids = [
        lax.rem(my_x + i, nx) * 2 + lax.rem(my_core + c, 2)
        for i in both_ways(nx)
        for c in range(2)
    ]
    owners = [lax.rem(owner + i, m) for i in range(m)]
    base = [lax.div(p, 2) * (2 * nz) + lax.rem(p, 2) for p in plane_ids]

    def there(i, j):
        return {"chan": base[i] + 2 * line[j]}

    on_line = [there(0, j) for j in range(nz)]
    in_plane = [there(i, 0) for i in range(np_)]
    in_column = [{"src": y} for y in owners]

    barrier = pltpu.get_barrier_semaphore()
    for devices in (on_line, in_plane, in_column):
        for device in devices[1:]:
            pl.semaphore_signal(barrier, inc=1, device_id=device, device_id_type=MESH)

    def spread(places, devices, send, recv, send_sem, recv_sem):
        mine = places[0]
        for place, device in zip(places[1:], devices[1:]):
            pltpu.make_async_remote_copy(
                src_ref=send(place),
                dst_ref=recv.at[mine],
                send_sem=send_sem,
                recv_sem=recv_sem,
                device_id=device,
                device_id_type=MESH,
            ).start()
        pltpu.make_async_copy(send(mine), recv.at[mine], recv_sem).start()

    def arrived(recv, sem):
        pltpu.make_async_copy(recv, recv, sem).wait()

    def left(recv, sem):
        some = recv.at[pl.ds(0, recv.shape[0] - 1)]
        pltpu.make_async_copy(some, some, sem).wait()

    def spread_z(send, recv, send_sem, recv_sem):
        spread(line, on_line, send, recv, send_sem, recv_sem)

    def spread_x(send, recv, send_sem, recv_sem):
        spread(plane_ids, in_plane, send, recv, send_sem, recv_sem)

    ZMETA, XMETA, SRC1, SRC2, SRC3, SRC4, MIS, FLAG = range(8)

    diagonal = iota((pairs, pairs), 0) == iota((pairs, pairs), 1)
    earlier = iota((pairs, pairs), 0) < iota((pairs, pairs), 1)
    group = group_ref[...]
    group_col = jnp.sum(jnp.where(diagonal, group, 0), axis=1, keepdims=True)
    rank = jnp.sum(jnp.where((group_col == group) & earlier, 1, 0), axis=0, keepdims=True)
    slab = lax.rem(group >> 1, nz)
    slab_col = lax.rem(group_col >> 1, nz)
    place = jnp.sum(jnp.where((slab_col == slab) & earlier, 1, 0), axis=0, keepdims=True)
    plane = lax.div(group, 2 * nz) * 2 + (group & 1)
    over = jnp.max(jnp.where(place >= room, 1.0, 0.0), axis=1, keepdims=True)
    row = jnp.where(place < room, slab * room + place, -1)
    pick = ones_where(row == iota((z_rows, pairs), 0))
    pick_bf = jnp.concatenate([pick, pick], axis=1).astype(BF16)

    def pack(q):
        block = jnp.concatenate(
            [
                obs_ref[:, q * PART : (q + 1) * PART],
                obs_ref[:, bins + q * PART : bins + (q + 1) * PART],
            ],
            axis=1,
        )
        values = dot(pick_bf, jnp.concatenate(halves(block), axis=0))
        z_send[q, :, 0:room, :] = values[:, :PART].reshape(nz, room, PART)
        z_send[q, :, room : 2 * room, :] = values[:, PART:].reshape(nz, room, PART)

    def send_z(q):
        spread_z(lambda z: z_send.at[q, z], z_recv.at[q], zs_sem.at[q], zr_sem.at[q])

    pack(0)
    pack(1)
    lane_z = iota((z_rows, 128), 1)
    rank_z = lax.rem(iota((z_rows, 128), 0), room)

    def along(values):
        return jnp.sum(jnp.where(pick > 0.5, values.astype(F32), 0.0), axis=1, keepdims=True)

    coded = (
        jnp.where(lane_z == rank_z, along(plane * CAP + rank + 1), 0.0)
        + jnp.where(lane_z == rank_z + 32, along(prec_ref[...]), 0.0)
        + jnp.where(lane_z == rank_z + 64, along(psrc_ref[...]), 0.0)
    )
    fold_z = one_hot(
        iota((nz, z_rows), 0) == lax.div(iota((nz, z_rows), 1), room)
    )
    zmeta = dot(fold_z, coded.astype(BF16)) + jnp.where(iota((nz, 128), 1) == 100, over, 0.0)
    zmeta_send[...] = zmeta.reshape(nz, 1, 128)

    half = time_len // 2
    steps = half // STEP
    digit = iota((32, bins), 0) >> 3
    times = (iota((32, bins), 0) & 7) * jnp.where(
        digit == 0, 1, jnp.where(digit == 1, 8, jnp.where(digit == 2, 64, 512))
    )
    phase = ((K0 + iota((32, bins), 1)) * times) & (2 * time_len - 1)
    angle = phase.astype(F32) * (math.pi / time_len)
    cos_d, sin_d = jnp.cos(angle), -jnp.sin(angle)
    for j in range(8):
        cj, sj = cos_d[8 + j : 9 + j], sin_d[8 + j : 9 + j]
        cos_b[8 * j : 8 * j + 8, :] = cj * cos_d[:8] - sj * sin_d[:8]
        sin_b[8 * j : 8 * j + 8, :] = sj * cos_d[:8] + cj * sin_d[:8]
    for j in range(steps // 8):
        cj, sj = cos_d[24 + j : 25 + j], sin_d[24 + j : 25 + j]
        cos_a[8 * j : 8 * j + 8] = (cj * cos_d[16:24] - sj * sin_d[16:24]).reshape(8, 1, bins)
        sin_a[8 * j : 8 * j + 8] = (sj * cos_d[16:24] + cj * sin_d[16:24]).reshape(8, 1, bins)

    turn = iota((1, PART), 1) & 3
    keep = jnp.where(turn == 0, 1.0, jnp.where(turn == 2, -1.0, 0.0))
    swap = jnp.where(turn == 1, 1.0, jnp.where(turn == 3, -1.0, 0.0))
    rec_halves[0:chans, :] = rec_ref[:, 0:half]
    rec_halves[chans : 2 * chans, :] = rec_ref[:, half:time_len]

    def fill(i, carry):
        at = pl.ds(pl.multiple_of(i * STEP, STEP), STEP)
        for q in range(chunks):
            part = slice(q * PART, (q + 1) * PART)
            ca, sa = cos_a[i, :, part], sin_a[i, :, part]
            cb, sb = cos_b[:, part], sin_b[:, part]
            tables[q][at, 0:PART] = (ca * cb - sa * sb).astype(BF16)
            tables[q][at, PART : 2 * PART] = (sa * cb + ca * sb).astype(BF16)
        return carry

    lax.fori_loop(0, steps, fill, 0)

    pl.semaphore_wait(barrier, nz - 1 + np_ - 1 + m - 1)

    spread_z(lambda z: zmeta_send.at[z], zmeta_recv, small_s.at[ZMETA], small_r.at[ZMETA])
    send_z(0)
    send_z(1)

    power = jnp.zeros((chans, 1), F32)
    for q in range(chunks):
        sums = dot(rec_halves[...], tables[q][...])
        late_re, late_im = sums[chans:, :PART], sums[chans:, PART:]
        values = sums[:chans] + jnp.concatenate(
            [keep * late_re + swap * late_im, keep * late_im - swap * late_re], axis=1
        )
        spec[:, 2 * q * PART : 2 * (q + 1) * PART] = values
        power = power + jnp.sum(values * values, axis=1, keepdims=True)
    norm = jnp.sqrt(power / bins + 1e-6)

    wanted = jnp.sum(
        jnp.where(iota((sources, sources), 0) == iota((sources, sources), 1), vs_ref[...], 0),
        axis=1,
        keepdims=True,
    )
    chosen = one_hot(iota((sources, chans), 1) == wanted - me * chans)
    for q in range(chunks):
        pair = halves(spec[:, 2 * q * PART : (2 * q + 2) * PART] / norm)
        white[q, 0:chans, :], white[q, chans : 2 * chans, :] = pair
        src_send[q] = dot2(chosen, pair)

    spread_x(lambda p: src_send.at[p], src_mid, small_s.at[SRC1], small_r.at[SRC1])
    for q in range(2, chunks):
        pack(q)

    def forward_x(q):
        arrived(z_recv.at[q], zr_sem.at[q])
        block = jnp.concatenate(
            [
                z_recv[q, :, 0:room, :].reshape(z_rows, PART),
                z_recv[q, :, room : 2 * room, :].reshape(z_rows, PART),
            ],
            axis=1,
        )
        values = dot2(perm_ref[...], halves(block))
        x_send[q, :, 0:plane_slots, :] = values[:, :PART].reshape(np_, plane_slots, PART)
        x_send[q, :, plane_slots : 2 * plane_slots, :] = values[:, PART:].reshape(
            np_, plane_slots, PART
        )
        spread_x(lambda p: x_send.at[q, p], x_recv.at[q], xs_sem.at[q], xr_sem.at[q])

    def name_slots():
        arrived(xmeta_recv, small_r.at[XMETA])
        unfold_x = one_hot(lax.div(iota((slots, np_), 0), plane_slots) == iota((slots, np_), 1))
        metas = xmeta_recv[...].reshape(np_, 128)
        flag_send[...] = jnp.broadcast_to(
            jnp.max(jnp.where(iota((np_, 128), 1) == 100, metas, 0.0), keepdims=True), (1, 128)
        )
        spread(owners, in_column, lambda y: flag_send, flag_recv, small_s.at[FLAG], small_r.at[FLAG])
        wide = dot(unfold_x, metas.astype(BF16))
        lane_x = lax.rem(iota((slots, 128), 0), plane_slots)
        receiver = lanes_of(wide, lane_x).astype(jnp.int32) - 1
        source = lanes_of(wide, lane_x + plane_slots).astype(jnp.int32)
        hits = ones_where(iota((slots, chans), 1) == receiver)
        g_ref[:, 0:chans] = hits.astype(BF16)
        g_ref[:, chans : 2 * chans] = hits.astype(BF16)
        gt_ref[...] = hits.T.astype(BF16)
        named = lax.rem(iota((slots, 2 * sources), 1), sources) == source
        h_ref[...] = one_hot(named & (receiver >= 0))

    arrived(src_mid, small_r.at[SRC1])
    part = jnp.sum(src_mid[...], axis=0)
    few = sources // nz
    for z in range(nz):
        src_part[z] = part[z * few : (z + 1) * few]
    spread_z(lambda z: src_part.at[z], src_line, small_s.at[SRC2], small_r.at[SRC2])
    send_z(2)

    arrived(zmeta_recv, small_r.at[ZMETA])
    unfold_z = one_hot(lax.div(iota((z_rows, nz), 0), room) == iota((z_rows, nz), 1))
    metas = zmeta_recv[...].reshape(nz, 128)
    line_over = jnp.max(jnp.where(iota((nz, 128), 1) == 100, metas, 0.0), keepdims=True)
    wide = dot(unfold_z, metas.astype(BF16))
    code = lanes_of(wide, rank_z).astype(jnp.int32) - 1
    came_from = lax.div(iota((z_rows, 1), 0), room)
    to_plane = jnp.where(code >= 0, code >> 2, -1)
    within = came_from * CAP + (code & 3)
    target = jnp.where(code >= 0, to_plane * plane_slots + within, -1)
    perm_ref[...] = ones_where(iota((z_rows, slots), 1) == target).T.astype(BF16)
    to_plane_hot = ones_where(iota((z_rows, 128), 1) == to_plane)
    coded = jnp.where(lane_z == within, lanes_of(wide, rank_z + 32) + 1.0, 0.0) + jnp.where(
        lane_z == within + plane_slots, lanes_of(wide, rank_z + 64), 0.0
    )
    xmeta = dot(to_plane_hot.T[:np_].astype(BF16), coded.astype(BF16)) + jnp.where(
        iota((np_, 128), 1) == 100, line_over, 0.0
    )
    xmeta_send[...] = xmeta.reshape(np_, 1, 128)
    spread_x(lambda p: xmeta_send.at[p], xmeta_recv, small_s.at[XMETA], small_r.at[XMETA])

    arrived(src_line, small_r.at[SRC2])
    src_own[...] = jnp.sum(src_line[...], axis=0)
    spread_z(lambda z: src_own, src_rows, small_s.at[SRC3], small_r.at[SRC3])
    send_z(3)
    forward_x(0)
    forward_x(1)
    name_slots()
    arrived(src_rows, small_r.at[SRC3])
    src_all[...] = jnp.concatenate([src_rows[z] for z in range(nz)], axis=0)
    spread_x(lambda p: src_all, src_recv, small_s.at[SRC4], small_r.at[SRC4])
    for q in range(4, min(6, chunks)):
        send_z(q)
    forward_x(2)
    arrived(src_recv, small_r.at[SRC4])

    mis_acc[...] = jnp.zeros_like(mis_acc)

    def correlate(q):
        arrived(x_recv.at[q], xr_sem.at[q])
        band = (q * PART + iota((1, PART), 1)).astype(F32)
        taper = 0.5 - 0.5 * jnp.cos((band + 0.5) * (2.0 * math.pi / bins))
        source_rows = dot(h_ref[...], jnp.concatenate(halves(src_recv[q]), axis=0))
        receiver_rows = dot(g_ref[...], white[q])
        s_re, s_im = source_rows[:, :PART], source_rows[:, PART:]
        r_re, r_im = receiver_rows[:, :PART], receiver_rows[:, PART:]
        d_re = s_re * r_re + s_im * r_im - x_recv[q, :, 0:plane_slots, :].reshape(slots, PART)
        d_im = s_re * r_im - s_im * r_re - x_recv[q, :, plane_slots : 2 * plane_slots, :].reshape(
            slots, PART
        )
        e_re, e_im = taper * d_re, taper * d_im
        mis_acc[...] += e_re * d_re + e_im * d_im
        terms = jnp.concatenate([e_re * s_re - e_im * s_im, e_re * s_im + e_im * s_re], axis=1)
        adj_send[q] = dot2(gt_ref[...], halves(terms)).reshape(m, rows_out, 2 * PART)
        spread(
            owners,
            in_column,
            lambda y: adj_send.at[q, y],
            adj_recv.at[q],
            ys_sem.at[q],
            yr_sem.at[q],
        )

    def inverse(q):
        arrived(adj_recv.at[q], yr_sem.at[q])
        total = adj_recv[q, 0]
        for y in range(1, m):
            total = total + adj_recv[q, y]
        total = total * (1.0 / math.sqrt(bins))
        real, imaginary = total[:, :PART], total[:, PART:]
        late = jnp.concatenate(
            [keep * real - swap * imaginary, swap * real + keep * imaginary], axis=1
        )
        both = jnp.concatenate(halves(jnp.concatenate([total, late], axis=0)), axis=0)
        span = min(512, half)

        def one(i, carry):
            at = pl.ds(pl.multiple_of(i * span, span), span)
            after = pl.ds(pl.multiple_of(half + i * span, span), span)
            product = dot_t(both, tables[q][at, :])
            values = product[: 2 * rows_out] + product[2 * rows_out :]
            if q == 0:
                out_ref[:, at] = values[:rows_out]
                out_ref[:, after] = values[rows_out:]
            else:
                out_ref[:, at] += values[:rows_out]
                out_ref[:, after] += values[rows_out:]
            return carry

        lax.fori_loop(0, half // span, one, 0)

    for q in range(chunks):
        if q + 6 < chunks:
            send_z(q + 6)
        correlate(q)
        if q + 3 < chunks:
            forward_x(q + 3)
        if 3 <= q < chunks - 1:
            inverse(q - 3)

    lane_4 = iota((slots, 128), 0) & 3
    total = jnp.sum(mis_acc[...], axis=1, keepdims=True) * (0.5 / bins)
    count = nz * np_
    fold_4 = one_hot(iota((count, slots), 0) == (iota((count, slots), 1) >> 2))
    spread_out = jnp.where(iota((slots, 128), 1) == lane_4, total, 0.0)
    mis_send[...] = dot2(fold_4, halves(spread_out)).reshape(count, 1, 128)

    spread(
        [plane_ids[i] * nz + line[j] for i in range(np_) for j in range(nz)],
        [there(i, j) for i in range(np_) for j in range(nz)],
        lambda u: mis_send.at[u],
        mis_recv,
        small_s.at[MIS],
        small_r.at[MIS],
    )
    for q in range(max(0, chunks - 4), chunks):
        inverse(q)

    arrived(mis_recv, small_r.at[MIS])
    unfold_4 = one_hot((iota((slots, count), 0) >> 2) == iota((slots, count), 1))
    back = dot2(unfold_4, halves(mis_recv[...].reshape(count, 128)))
    own = ones_where((plane * nz + slab) * CAP + rank == iota((slots, pairs), 0))
    mis_ref[...] = jnp.sum(own * lanes_of(back, lane_4), axis=0)
    arrived(flag_recv, small_r.at[FLAG])
    over_ref[...] = jnp.max(flag_recv[...], axis=0)

    for q in range(chunks):
        left(z_recv.at[q], zs_sem.at[q])
        left(x_recv.at[q], xs_sem.at[q])
        left(adj_recv.at[q], ys_sem.at[q])
    for recv, sem in (
        (zmeta_recv, ZMETA),
        (xmeta_recv, XMETA),
        (src_mid, SRC1),
        (src_line, SRC2),
        (src_rows, SRC3),
        (src_recv, SRC4),
        (mis_recv, MIS),
        (flag_recv, FLAG),
    ):
        left(recv, small_s.at[sem])


def exchange(nz, np_, m, room, number, operands):
    records, observed = operands[0], operands[5]
    chans, time_len = records.shape
    pairs, width = observed.shape
    bins = width // 2
    chunks = bins // PART
    rows_out = chans // m
    sources = operands[1].shape[1]
    slots = np_ * nz * CAP
    assert chunks == np_
    vmem = pltpu.VMEM
    return pl.pallas_call(
        functools.partial(kernel, nz, np_, m, room),
        out_shape=(
            jax.ShapeDtypeStruct((rows_out, time_len), F32),
            jax.ShapeDtypeStruct((pairs,), F32),
            jax.ShapeDtypeStruct((1, 128), F32),
        ),
        in_specs=[pl.BlockSpec(memory_space=vmem)] * 6,
        out_specs=(pl.BlockSpec(memory_space=vmem),) * 3,
        scratch_shapes=[
            vmem((chunks, nz, 2 * room, PART), F32),
            vmem((chunks, nz, 2 * room, PART), F32),
            vmem((chunks, np_, 2 * nz * CAP, PART), F32),
            vmem((chunks, np_, 2 * nz * CAP, PART), F32),
            vmem((nz, 1, 128), F32),
            vmem((nz, 1, 128), F32),
            vmem((np_, 1, 128), F32),
            vmem((np_, 1, 128), F32),
            vmem((np_, sources, 2 * PART), F32),
            vmem((np_, sources, 2 * PART), F32),
            vmem((nz, sources // nz, 2 * PART), F32),
            vmem((nz, sources // nz, 2 * PART), F32),
            vmem((sources // nz, 2 * PART), F32),
            vmem((nz, sources // nz, 2 * PART), F32),
            vmem((sources, 2 * PART), F32),
            vmem((np_, sources, 2 * PART), F32),
            vmem((chunks, m, rows_out, 2 * PART), F32),
            vmem((chunks, m, rows_out, 2 * PART), F32),
            vmem((nz * np_, 1, 128), F32),
            vmem((nz * np_, 1, 128), F32),
            vmem((1, 128), F32),
            vmem((m, 1, 128), F32),
            vmem((2 * chans, time_len // 2), BF16),
            [vmem((time_len // 2, 2 * PART), BF16) for _ in range(chunks)],
            vmem((time_len // 2 // STEP, 1, bins), F32),
            vmem((time_len // 2 // STEP, 1, bins), F32),
            vmem((STEP, bins), F32),
            vmem((STEP, bins), F32),
            vmem((chans, width), F32),
            vmem((chunks, 2 * chans, 2 * PART), BF16),
            vmem((slots, nz * room), BF16),
            vmem((slots, 2 * chans), BF16),
            vmem((chans, slots), BF16),
            vmem((slots, 2 * sources), BF16),
            vmem((slots, PART), F32),
            pltpu.SemaphoreType.DMA((chunks,)),
            pltpu.SemaphoreType.DMA((chunks,)),
            pltpu.SemaphoreType.DMA((chunks,)),
            pltpu.SemaphoreType.DMA((chunks,)),
            pltpu.SemaphoreType.DMA((chunks,)),
            pltpu.SemaphoreType.DMA((chunks,)),
            pltpu.SemaphoreType.DMA((8,)),
            pltpu.SemaphoreType.DMA((8,)),
        ],
        compiler_params=pltpu.CompilerParams(
            collective_id=number, has_side_effects=True, vmem_limit_bytes=56 * 1024 * 1024
        ),
    )(*operands)


def per_device(n, m, records, virtual_sources, pair_group, pair_receiver, pair_source, observed):
    pairs, width = observed.shape
    np_ = width // 2 // PART
    nz = n // np_
    most = np_ * CAP
    usual = max(8, most * 3 // 4 // 8 * 8)
    operands = (
        records,
        virtual_sources.reshape(1, -1),
        pair_group.reshape(1, pairs),
        pair_receiver.reshape(1, pairs),
        pair_source.reshape(1, pairs),
        observed,
    )
    adjoint, misfit, over = exchange(nz, np_, m, usual, 0, operands)
    adjoint, misfit = lax.cond(
        over[0, 0] > 0.0,
        lambda held: exchange(nz, np_, m, most, 1, operands)[:2],
        lambda held: held,
        (adjoint, misfit),
    )
    return adjoint, misfit


def solution(mesh):
    return jax.shard_map(
        functools.partial(per_device, mesh.shape["chan"], mesh.shape["src"]),
        mesh=mesh,
        in_specs=(
            P("chan", None),
            P("src"),
            P(("chan", "src"), None),
            P(("chan", "src")),
            P(("chan", "src")),
            P(("chan", "src"), None),
        ),
        out_specs=(P(("chan", "src"), None), P(("chan", "src"))),
        check_vma=False,
    )
```
